256 devices in a mesh: seq: 32 (over y, x, core), head: 4 (over z_lo), dp: 2 (over z_hi).
Axes of the slice: x: 4, y: 4, z: 8 (z_hi: 2, z_lo: 4; z = z_hi * 4 + z_lo), core: 2. Of those that a mesh axis runs over, the one named last changes fastest.
Arguments:
- tokens: bfloat16 [8192, 4096], P(('dp', 'seq'), 'head'), parts along dimension 0, may hold values from -60 to 60
- w_key: bfloat16 [4096, 4096], P('seq', 'head'), may hold values from -0.09375 to 0.09375
- w_value: bfloat16 [4096, 4096], P('seq', 'head'), may hold values from -0.09375 to 0.09375
- w_query: bfloat16 [4096, 4096], P('seq', 'head'), may hold values from -0.1875 to 0.1875
- slot_queries: bfloat16 [512, 4096], P('dp', 'head'), parts along dimension 0, may hold values from -100 to 100
- memory: bfloat16 [512, 4096], P('dp', 'head'), parts along dimension 0, may hold values from -6 to 6
- norm_gain: float32 [4096], P('head'), may hold values from 0.5 to 1.5
- doc_length: int32 [2], P('dp'), parts along dimension 0, may hold values from 1024 to 4096
Outputs:
- unpacked: bfloat16 [8192, 4096], P(('dp', 'seq'), 'head'), parts along dimension 0
- new_memory: bfloat16 [512, 4096], P('dp', 'head'), parts along dimension 0
The draws below stay inside these ranges and needn't reach their ends.
There are 2 independent parts, one for each index of `dp`. The reference program is written for one: setup_inputs(seed, part) draws one part's arguments, and reference() takes and returns one part's arrays. A program takes and returns all parts, laid end to end along the dimension named above; an argument that names none is the same for every part. Nothing has to cross between parts.
All inputs are finite; a program needn't handle non-finite values.
Results may differ from the reference program's by a relative error of at most 0.003.
The reference program's roundings to bfloat16 on the way count: a program that leaves them out, or rounds other values in their place, can miss the bound.
Values may be sent and summed in bfloat16 or wider, within the bound.
A program may use at most 192 MiB of HBM per device.

```python
import math
import jax
import jax.numpy as jnp
from jax import lax

D = 4096
HEADS = 32
HEAD_DIM = 128
SLOTS = 256
SEQ = 4096


def draw_tokens(key, part):
    key = jax.random.fold_in(key, 11)
    key_base = jax.random.fold_in(key, 0)
    result = jnp.clip(jax.random.normal(key_base, (SEQ, D), jnp.float32), -5.5, 5.5)
    return result.astype(jnp.bfloat16)


def draw_slot_queries(key, part):
    key = jax.random.fold_in(key, 23)
    key_base, key_rows = jax.random.split(key, 2)
    row_scale = jnp.exp(jax.random.uniform(key_rows, (SLOTS, 1), jnp.float32, math.log(0.8), math.log(3.5)))
    result = jnp.clip(jax.random.normal(key_base, (SLOTS, D), jnp.float32), -4.0, 4.0) * row_scale
    return result.astype(jnp.bfloat16)


def draw_memory(key, part):
    key = jax.random.fold_in(key, 37)
    key_base, key_cols = jax.random.split(key, 2)
    column_scale = 3.0 ** (jnp.arange(D, dtype=jnp.float32) / D)
    column_scale = column_scale * jnp.exp(jax.random.uniform(key_cols, (1, D), jnp.float32, math.log(0.5), math.log(2.0)))
    base = jnp.clip(jax.random.normal(key_base, (SLOTS, D), jnp.float32), -4.0, 4.0) * 0.25
    result = jnp.clip(base * column_scale, -6.0, 6.0)
    return result.astype(jnp.bfloat16)


def level_of(own_key, shape, pieces, low, largest):
    loudness, own = 1.0, jax.random.fold_in(own_key, 6)
    for position, blocks in pieces:
        draws = jnp.exp(jax.random.uniform(jax.random.fold_in(own, position), (blocks,), jnp.float32, low / len(pieces), largest / len(pieces)))
        loudness = loudness * jnp.repeat(draws, shape[position] // blocks).reshape([-1 if axis == position else 1 for axis in range(len(shape))])
    return loudness


def noise(own_key, extent, width, bound, shards=(), kind=jnp.bfloat16):
    values = width * jax.random.normal(own_key, extent, jnp.float32)
    if shards:
        values = values * level_of(own_key, extent, shards, -0.22, 0.18)
    return jnp.clip(values, -bound, bound).astype(kind)


def setup_inputs(seed: int = 0, part: int = 0) -> dict:
    seeds = jax.random.split(jax.random.key(seed), 9)
    part_keys = jax.random.split(jax.random.fold_in(seeds[8], part), 9)
    tokens = draw_tokens(jax.random.fold_in(jax.random.fold_in(seeds[8], part), 71), part)
    w_key = noise(seeds[1], (D, D), D ** -0.5, 0.09375, ((0, 32), (1, 4)))
    w_value = noise(seeds[2], (D, D), D ** -0.5, 0.09375, ((0, 32), (1, 4)))
    w_query = noise(seeds[3], (D, D), (D // 4) ** -0.5, 0.1875, ((0, 32), (1, 4)))
    slot_queries = draw_slot_queries(jax.random.fold_in(jax.random.fold_in(seeds[8], part), 71), part)
    memory = draw_memory(jax.random.fold_in(jax.random.fold_in(seeds[8], part), 71), part)
    norm_gain = jnp.clip(1.0 + 0.1 * jax.random.normal(seeds[6], (D,), jnp.float32), 0.5, 1.5)
    doc_length = jax.random.randint(part_keys[7], (1,), SEQ // 4, SEQ + 1).astype(jnp.int32)
    return dict(tokens=tokens, w_key=w_key, w_value=w_value, w_query=w_query, slot_queries=slot_queries, memory=memory, norm_gain=norm_gain, doc_length=doc_length)


NEGATIVE = -1e+30
EPSILON = 1e-05

def split_heads(matrix, count):
    return matrix.reshape(count, HEADS, HEAD_DIM).transpose(1, 0, 2)

def reference(tokens, w_key, w_value, w_query, slot_queries, memory, norm_gain, doc_length):
    scaling = 1.0 / math.sqrt(HEAD_DIM)
    key_full = jnp.dot(tokens, w_key, preferred_element_type=jnp.float32).astype(jnp.bfloat16)
    value_full = jnp.dot(tokens, w_value, preferred_element_type=jnp.float32).astype(jnp.bfloat16)
    query_full = jnp.dot(tokens, w_query, preferred_element_type=jnp.float32).astype(jnp.bfloat16)
    validity = jnp.arange(SEQ) < doc_length[0]

    def pack_head(operands):
        query_head, key_head, value_head = operands
        scores = jnp.dot(query_head, key_head.T, preferred_element_type=jnp.float32) * scaling
        scores = jnp.where(validity[None, :], scores, NEGATIVE)
        highest = lax.optimization_barrier(jnp.max(scores, axis=1, keepdims=True))
        weights = jnp.where(validity[None, :], jnp.exp(scores - highest), 0.0)
        denominator = lax.optimization_barrier(jnp.sum(weights, axis=1, keepdims=True))
        summed = jnp.dot(weights, value_head.astype(jnp.float32), precision=lax.Precision.HIGHEST)
        return summed / denominator
    packed = lax.map(pack_head, (split_heads(slot_queries, SLOTS), split_heads(key_full, SEQ), split_heads(value_full, SEQ)))
    packed = packed.transpose(1, 0, 2).reshape(SLOTS, D)
    combined = memory.astype(jnp.float32) + packed
    row_mean = lax.optimization_barrier(jnp.sum(combined, axis=1, keepdims=True)) / D
    row_square = lax.optimization_barrier(jnp.sum(combined * combined, axis=1, keepdims=True)) / D
    inverse = lax.rsqrt(row_square - row_mean * row_mean + EPSILON)
    new_memory = ((combined - row_mean) * inverse * norm_gain[None, :]).astype(jnp.bfloat16)

    def unpack_head(operands):
        query_head, memory_head = operands
        scores = jnp.dot(query_head, memory_head.T, preferred_element_type=jnp.float32) * scaling
        probs = jax.nn.softmax(scores, axis=-1).astype(jnp.bfloat16)
        return jnp.dot(probs, memory_head, preferred_element_type=jnp.float32)
    outputs = lax.map(unpack_head, (split_heads(query_full, SEQ), split_heads(new_memory, SLOTS)))
    outputs = outputs.transpose(1, 0, 2).reshape(SEQ, D)
    unpacked = jnp.where(validity[:, None], outputs, 0.0).astype(jnp.bfloat16)
    return (unpacked, new_memory)
```

```python
import math

import jax
import jax.numpy as jnp
from jax import lax
from jax.experimental import pallas as pl
from jax.experimental.pallas import tpu as pltpu
from jax.sharding import PartitionSpec as P

D = 4096
HEAD_DIM = 128
NEGATIVE = -1e30
EPSILON = 1e-05
SCALING = 1.0 / math.sqrt(HEAD_DIM)
MESH = pl.DeviceIdType.MESH
F32 = jnp.float32
BF16 = jnp.bfloat16
NT = (((1,), (1,)), ((), ()))


def merge(pieces):
    outs, stats = [], []
    for h in range(2):
        tops = [p[:, 256 + 2 * h : 257 + 2 * h] for p in pieces]
        sums = [p[:, 257 + 2 * h : 258 + 2 * h] for p in pieces]
        accs = [p[:, h * 128 : (h + 1) * 128] for p in pieces]
        top = tops[0]
        for t in tops[1:]:
            top = jnp.maximum(top, t)
        factors = [jnp.exp(t - top) for t in tops]
        total = sum(s * f for s, f in zip(sums, factors))
        acc = sum(a * f for a, f in zip(accs, factors))
        outs.append(acc)
        stats.append((top, total))
    return outs, stats


def stat_lanes(stats, rows):
    lane = lax.broadcasted_iota(jnp.int32, (rows, 128), 1)
    (m0, s0), (m1, s1) = stats
    return jnp.where(lane == 0, m0, jnp.where(lane == 1, s0, jnp.where(lane == 2, m1, s1)))


def kernel(
    tok, wk, wv, wq, sq, mem, gain, dl,
    o_un, o_nm,
    tokb, wb, sqb, memb, acc, pm, pr, mg, mr, st, nmf, ob,
    loc, z_s, z_r, zb_s, zb_r, xa_s, xa_r, f_s, f_r, xw_s, xw_r, yw_s, yw_r, cw_s, cw_r,
    p1, p2_s, p2_r, p3_s, p3_r, p4_s, p4_r, n_s, n_r, nc_s, nc_r, u_s, u_r,
):
    seq = lax.axis_index("seq")
    z = lax.axis_index("head")
    dp = lax.axis_index("dp")
    y, x, c = seq // 8, (seq // 2) % 4, seq % 2
    xs = [(x + d) % 4 for d in range(4)]
    ys = [(y + d) % 4 for d in range(4)]
    zs = [(z + d) % 4 for d in range(4)]

    def dev(x=x, y=y, z=z, c=c):
        return (y * 8 + x * 2 + c, z, dp)

    def remote(src, dst, send, recv, to):
        return pltpu.make_async_remote_copy(
            src_ref=src, dst_ref=dst, send_sem=send, recv_sem=recv, device_id=to,
            device_id_type=MESH,
        )

    sib = dev(c=1 - c)
    ws = (wk, wv, wq)

    def cols(i):
        return pl.ds(pl.multiple_of(i * 256, 256), 256)

    def group(i):
        return pl.ds(pl.multiple_of(i * 128, 128), 128)

    slots = pl.ds(pl.multiple_of(y * 64 + c * 32, 32), 32)
    local = [
        pltpu.make_async_copy(tok, tokb.at[z, group(x)], loc.at[0]),
        pltpu.make_async_copy(sq.at[:, cols(x)], sqb, loc.at[1]),
        pltpu.make_async_copy(mem.at[slots, cols(x)], memb, loc.at[2]),
    ]
    for m in range(3):
        local.append(
            pltpu.make_async_copy(ws[m].at[:, cols(x)], wb.at[m, y, x, c], loc.at[3 + m])
        )
    for cp in local:
        cp.start()

    partners = [sib]
    for d in range(1, 4):
        partners += [dev(y=ys[d]), dev(y=ys[d], c=1 - c)]
    for dx in range(4):
        for dz in range(4):
            if dx or dz:
                partners.append(dev(x=xs[dx], z=zs[dz]))
    barrier = pltpu.get_barrier_semaphore()
    for p in partners:
        pl.semaphore_signal(barrier, inc=1, device_id=p, device_id_type=MESH)
    pl.semaphore_wait(barrier, len(partners))

    sent = []

    def go(cp):
        cp.start()
        sent.append(cp)

    first = 1 + z % 2
    third = 3 * (1 - z // 2)
    second = 6 - z - first - third
    order = [z, first, second, third]
    onward = [None, 3 * (z // 2), 3 - z, 3 * (z // 2)]
    middle = (z + 1) // 2 == 1

    def chain(i, src_of, send, recv):
        if i == 0:
            ref = src_of(z)
            up = remote(ref, ref, send.at[0], recv.at[z], dev(z=z + 1))
            down = remote(ref, ref, send.at[1], recv.at[z], dev(z=z - 1))
            return [(z < 3, up), (z > 0, down)]
        zi = order[i]
        ref = src_of(zi)
        return [(middle, remote(ref, ref, send.at[i + 1], recv.at[zi], dev(z=onward[i])))]

    def start_chain(*args):
        for cond, cp in chain(*args):
            pl.when(cond)(cp.start)

    def finish_chain(*args):
        for cond, cp in chain(*args):
            pl.when(cond)(cp.wait_send)

    def wait_chain(i, src_of, send, recv):
        ref = src_of(order[i])
        remote(ref, ref, send.at[0], recv.at[order[i]], sib).wait_recv()

    def own_x(zi):
        return tokb.at[zi, group(x)]

    def far_x(zi):
        return tokb.at[zi, group(xs[2])]

    A = (own_x, z_s, z_r)
    B = (far_x, zb_s, zb_r)

    def send_w(m):
        for d in range(1, 4):
            go(remote(ws[m].at[:, cols(xs[d])], wb.at[m, y, x, c], xw_s.at[m, d], xw_r.at[m, x],
                      dev(x=xs[d])))

    def send_x(i, src=None):
        zi = order[i]
        ref = own_x(zi)
        go(remote(ref, ref, xa_s.at[i, 0], xa_r.at[zi, 0], dev(x=xs[1])))
        go(remote(ref, ref, xa_s.at[i, 1], xa_r.at[zi, 1], dev(x=xs[3])))

    def wait_x(i):
        zi = order[i]
        for k, d in ((0, 3), (1, 1)):
            ref = tokb.at[zi, group(xs[d])]
            remote(ref, ref, xa_s.at[0, 0], xa_r.at[zi, k], sib).wait_recv()

    def spread_w(m):
        local[3 + m].wait()
        for d in range(1, 4):
            ref = wb.at[m, y, xs[d], c]
            remote(ref, ref, xw_s.at[m, d], xw_r.at[m, xs[d]], sib).wait_recv()
        ref = wb.at[m, y, :, c]
        for d in (2, 1, 3):
            go(remote(ref, ref, yw_s.at[m, d], yw_r.at[m, y], dev(y=ys[d])))
        go(remote(ref, ref, cw_s.at[m, 0], cw_r.at[m, y], sib))

    def pass_w(m):
        for d in (1, 3, 2):
            ref = wb.at[m, ys[d], :, c]
            remote(ref, ref, yw_s.at[m, d], yw_r.at[m, ys[d]], sib).wait_recv()
            go(remote(ref, ref, cw_s.at[m, d], cw_r.at[m, ys[d]], sib))

    def wait_w(m):
        for d in range(4):
            ref = wb.at[m, ys[d], :, 1 - c]
            remote(ref, ref, cw_s.at[m, d], cw_r.at[m, ys[d]], sib).wait_recv()

    def project(m, zi, fresh):
        w = wb[m, zi].reshape(1024, 256)
        r = jnp.dot(tokb[zi], w, preferred_element_type=F32)
        if fresh:
            acc[m] = r
        else:
            acc[m] += r

    send_w(0)
    local[0].wait()
    start_chain(0, *A)
    send_w(1)
    send_x(0)
    send_w(2)
    spread_w(0)
    wait_chain(1, *A)
    start_chain(1, *A)
    send_x(1)
    spread_w(1)
    wait_x(0)
    half = pl.ds(pl.multiple_of(xs[1] * 128, 64), 64)
    ref = tokb.at[z, half]
    go(remote(ref, ref, f_s.at[0], f_r.at[0], dev(x=xs[3])))
    half = pl.ds(pl.multiple_of(xs[3] * 128 + 64, 64), 64)
    ref = tokb.at[z, half]
    go(remote(ref, ref, f_s.at[1], f_r.at[1], dev(x=xs[1])))
    wait_chain(2, *A)
    start_chain(2, *A)
    send_x(2)
    spread_w(2)
    for k in range(2):
        ref = tokb.at[z, pl.ds(pl.multiple_of(xs[2] * 128 + 64 * k, 64), 64)]
        remote(ref, ref, f_s.at[k], f_r.at[k], sib).wait_recv()
    start_chain(0, *B)
    wait_chain(3, *A)
    start_chain(3, *A)
    send_x(3)
    pass_w(0)
    wait_chain(1, *B)
    start_chain(1, *B)
    pass_w(1)
    wait_w(0)
    wait_w(1)
    project(0, z, True)
    project(1, z, True)
    wait_chain(2, *B)
    start_chain(2, *B)
    wait_x(1)
    project(0, first, False)
    project(1, first, False)
    wait_chain(3, *B)
    start_chain(3, *B)
    wait_x(2)
    project(0, second, False)
    project(1, second, False)
    wait_x(3)
    project(0, third, False)
    project(1, third, False)

    local[1].wait()
    local[2].wait()
    length = dl[0]
    j = lax.broadcasted_iota(jnp.int32, (1, 512), 1)
    valid = y * 1024 + (j // 128) * 256 + c * 128 + j % 128 < length
    stats = []
    for h in range(2):
        hc = slice(h * 128, (h + 1) * 128)
        k = acc[0, :, hc].astype(BF16)
        v = acc[1, :, hc].astype(BF16)
        s = lax.dot_general(sqb[:, hc], k, NT, preferred_element_type=F32) * SCALING
        s = jnp.where(valid, s, NEGATIVE)
        top = jnp.max(s, axis=1, keepdims=True)
        p = jnp.where(valid, jnp.exp(s - top), 0.0)
        total = jnp.sum(p, axis=1, keepdims=True)
        high = p.astype(BF16)
        low = (p - high.astype(F32)).astype(BF16)
        a = jnp.dot(high, v, preferred_element_type=F32) + jnp.dot(
            low, v, preferred_element_type=F32
        )
        for yy in range(4):
            for cc in range(2):
                r = yy * 64 + cc * 32
                pm[cc, yy, :, hc] = a[r : r + 32]
        stats.append((top, total))
    lanes = stat_lanes(stats, 256)
    for yy in range(4):
        for cc in range(2):
            r = yy * 64 + cc * 32
            pm[cc, yy, :, 256:384] = lanes[r : r + 32]

    cp = remote(pm.at[1 - c], pr, p1.at[0], p1.at[1], sib)
    go(cp)
    cp.wait_recv()
    outs, stats = merge([pm[c].reshape(128, 384), pr[...].reshape(128, 384)])
    mg[:, :, 0:128] = outs[0].reshape(4, 32, 128)
    mg[:, :, 128:256] = outs[1].reshape(4, 32, 128)
    mg[:, :, 256:384] = stat_lanes(stats, 128).reshape(4, 32, 128)
    for d in (2, 1, 3):
        go(remote(mg.at[ys[d]], mr.at[y], p2_s.at[d], p2_r.at[y], dev(y=ys[d])))

    pass_w(2)
    wait_w(2)
    for i in range(4):
        project(2, i, i == 0)

    for d in range(1, 4):
        remote(mr.at[ys[d]], mr.at[ys[d]], p2_s.at[d], p2_r.at[ys[d]], sib).wait_recv()
    outs, stats = merge([mg[y]] + [mr[ys[d]] for d in range(1, 4)])
    packed = jnp.concatenate([outs[h] / stats[h][1] for h in range(2)], axis=1)
    combined = memb[...].astype(F32) + packed
    stacked = jnp.concatenate([combined, combined * combined, jnp.zeros((64, 256), F32)], axis=0)
    sums = lax.dot_general(
        jnp.ones((8, 256), F32), stacked, NT, precision=lax.Precision.HIGHEST,
        preferred_element_type=F32,
    )
    st[x, z] = sums
    for dz in (2, 3, 1, 0):
        for dx in (2, 1, 3, 0):
            if dx or dz:
                go(remote(st.at[x, z], st.at[x, z], p3_s.at[dx, dz], p3_r.at[x, z],
                          dev(x=xs[dx], z=zs[dz])))
    for dz in range(4):
        for dx in range(4):
            if dx or dz:
                ref = st.at[xs[dx], zs[dz]]
                remote(ref, ref, p3_s.at[dx, dz], p3_r.at[xs[dx], zs[dz]], sib).wait_recv()
    sums = jnp.sum(st[...].reshape(16, 8, 128), axis=0)
    column = jnp.transpose(sums)[:, 0:1] / D
    mean = column[0:32]
    square = column[32:64]
    inverse = lax.rsqrt(square - mean * mean + EPSILON)
    nmf[x, slots] = ((combined - mean) * inverse * gain[:, cols(x)]).astype(BF16)
    ref = nmf.at[x, slots]
    for d in (2, 1, 3):
        for cc in (0, 1):
            to = dev(y=ys[d], c=(c + cc) % 2)
            go(remote(ref, ref, p4_s.at[d, cc], p4_r.at[y, c], to))
    go(remote(ref, ref, p4_s.at[0, 1], p4_r.at[y, c], sib))

    for d in range(4):
        for cc in range(2):
            if d or cc:
                c2 = (c + cc) % 2
                ref = nmf.at[x, pl.ds(pl.multiple_of(ys[d] * 64 + c2 * 32, 32), 32)]
                remote(ref, ref, p4_s.at[d, cc], p4_r.at[ys[d], c2], sib).wait_recv()

    rows = pl.ds(pl.multiple_of(c * 128, 128), 128)
    ref = nmf.at[x, rows]
    for d in (2, 1, 3):
        go(remote(ref, ref, n_s.at[d], n_r.at[x], dev(x=xs[d])))

    r = lax.broadcasted_iota(jnp.int32, (128, 1), 0)
    final = []
    for d in (2, 1, 3, 0):
        g = xs[d]
        live = y * 1024 + g * 256 + c * 128 + r < length
        for h in range(2):
            hc = slice(h * 128, (h + 1) * 128)
            q = acc[2, group(g), hc].astype(BF16)
            n = nmf[x, :, hc]
            s = lax.dot_general(q, n, NT, preferred_element_type=F32) * SCALING
            e = jnp.exp(s - jnp.max(s, axis=1, keepdims=True))
            probs = (e / jnp.sum(e, axis=1, keepdims=True)).astype(BF16)
            o = jnp.dot(probs, n, preferred_element_type=F32)
            ob[g, :, hc] = jnp.where(live, o, 0.0).astype(BF16)
        if d:
            go(remote(ob.at[g], o_un.at[:, cols(x)], u_s.at[d], u_r.at[x], dev(x=g)))
        else:
            cp = pltpu.make_async_copy(ob.at[g], o_un.at[:, cols(x)], loc.at[6])
            cp.start()
            final.append(cp)

    for d in (1, 3, 2):
        ref = nmf.at[xs[d], rows]
        remote(ref, ref, n_s.at[d], n_r.at[xs[d]], sib).wait_recv()
        go(remote(ref, ref, nc_s.at[d], nc_r.at[xs[d]], sib))
    for d in (0, 1, 3, 2):
        if d:
            ref = nmf.at[xs[d], pl.ds(pl.multiple_of((1 - c) * 128, 128), 128)]
            remote(ref, ref, nc_s.at[d], nc_r.at[xs[d]], sib).wait_recv()
        cp = pltpu.make_async_copy(nmf.at[xs[d]], o_nm.at[:, cols(xs[d])], loc.at[7 + d])
        cp.start()
        final.append(cp)
    for d in range(1, 4):
        ref = o_un.at[:, cols(xs[d])]
        remote(ref, ref, u_s.at[d], u_r.at[xs[d]], sib).wait_recv()
    for cp in final:
        cp.wait()
    for cp in sent:
        cp.wait_send()
    for i in range(4):
        finish_chain(i, *A)
        finish_chain(i, *B)


def on_device(tokens, w_key, w_value, w_query, slot_queries, memory, norm_gain, doc_length):
    dma = pltpu.SemaphoreType.DMA
    anywhere = pl.BlockSpec(memory_space=pl.ANY)
    return pl.pallas_call(
        kernel,
        out_shape=(
            jax.ShapeDtypeStruct((128, 1024), BF16),
            jax.ShapeDtypeStruct((256, 1024), BF16),
        ),
        in_specs=[anywhere] * 6
        + [pl.BlockSpec(memory_space=pltpu.VMEM), pl.BlockSpec(memory_space=pltpu.SMEM)],
        out_specs=(anywhere, anywhere),
        scratch_shapes=[
            pltpu.VMEM((4, 512, 1024), BF16),
            pltpu.VMEM((3, 4, 4, 2, 128, 256), BF16),
            pltpu.VMEM((256, 256), BF16),
            pltpu.VMEM((32, 256), BF16),
            pltpu.VMEM((3, 512, 256), F32),
            pltpu.VMEM((2, 4, 32, 384), F32),
            pltpu.VMEM((4, 32, 384), F32),
            pltpu.VMEM((4, 32, 384), F32),
            pltpu.VMEM((4, 32, 384), F32),
            pltpu.VMEM((4, 4, 8, 128), F32),
            pltpu.VMEM((4, 256, 256), BF16),
            pltpu.VMEM((4, 128, 256), BF16),
            dma((11,)),
            dma((5,)),
            dma((4,)),
            dma((5,)),
            dma((4,)),
            dma((4, 2)),
            dma((4, 2)),
            dma((2,)),
            dma((2,)),
            dma((3, 4)),
            dma((3, 4)),
            dma((3, 4)),
            dma((3, 4)),
            dma((3, 4)),
            dma((3, 4)),
            dma((2,)),
            dma((4,)),
            dma((4,)),
            dma((4, 4)),
            dma((4, 4)),
            dma((4, 2)),
            dma((4, 2)),
            dma((4,)),
            dma((4,)),
            dma((4,)),
            dma((4,)),
            dma((4,)),
            dma((4,)),
        ],
        compiler_params=pltpu.CompilerParams(
            collective_id=0, has_side_effects=True, vmem_limit_bytes=40 * 2**20
        ),
        name="luna",
    )(
        tokens, w_key, w_value, w_query, slot_queries, memory, norm_gain.reshape(1, 1024),
        doc_length,
    )


def solution(mesh):
    in_specs = (
        P(("dp", "seq"), "head"),
        P("seq", "head"),
        P("seq", "head"),
        P("seq", "head"),
        P("dp", "head"),
        P("dp", "head"),
        P("head"),
        P("dp"),
    )
    out_specs = (P(("dp", "seq"), "head"), P("dp", "head"))
    return jax.shard_map(
        on_device, mesh=mesh, in_specs=in_specs, out_specs=out_specs, check_vma=False
    )
```

```python
import math

import jax
import jax.numpy as jnp
from jax import lax
from jax.experimental import pallas as pl
from jax.experimental.pallas import tpu as pltpu
from jax.sharding import PartitionSpec as P

D = 4096
HEAD_DIM = 128
NEGATIVE = -1e30
EPSILON = 1e-05
SCALING = 1.0 / math.sqrt(HEAD_DIM)
MESH = pl.DeviceIdType.MESH
F32 = jnp.float32
BF16 = jnp.bfloat16
NT = (((1,), (1,)), ((), ()))


def merge(pieces):
    outs, stats = [], []
    for h in range(2):
        tops = [p[:, 256 + 2 * h : 257 + 2 * h] for p in pieces]
        sums = [p[:, 257 + 2 * h : 258 + 2 * h] for p in pieces]
        accs = [p[:, h * 128 : (h + 1) * 128] for p in pieces]
        top = tops[0]
        for t in tops[1:]:
            top = jnp.maximum(top, t)
        factors = [jnp.exp(t - top) for t in tops]
        total = sum(s * f for s, f in zip(sums, factors))
        acc = sum(a * f for a, f in zip(accs, factors))
        outs.append(acc)
        stats.append((top, total))
    return outs, stats


def stat_lanes(stats, rows):
    lane = lax.broadcasted_iota(jnp.int32, (rows, 128), 1)
    (m0, s0), (m1, s1) = stats
    return jnp.where(lane == 0, m0, jnp.where(lane == 1, s0, jnp.where(lane == 2, m1, s1)))


def kernel(
    tok, wk, wv, wq, sq, mem, gain, dl,
    o_un, o_nm,
    tokb, wb, sqb, memb, gainb, dlb, acc, pm, pr, mg, mr, st, nmf, ob,
    loc, z_s, z_r, zb_s, zb_r, xa_s, xa_r, f_s, f_r, xw_s, xw_r, yw_s, yw_r, cw_s, cw_r,
    p1, p2_s, p2_r, p3_s, p3_r, p4_s, p4_r, n_s, n_r, nc_s, nc_r, u_s, u_r,
):
    seq = lax.axis_index("seq")
    z = lax.axis_index("head")
    dp = lax.axis_index("dp")
    y, x, c = seq // 8, (seq // 2) % 4, seq % 2
    xs = [(x + d) % 4 for d in range(4)]
    ys = [(y + d) % 4 for d in range(4)]
    zs = [(z + d) % 4 for d in range(4)]

    def dev(x=x, y=y, z=z, c=c):
        return (y * 8 + x * 2 + c, z, dp)

    def remote(src, dst, send, recv, to):
        return pltpu.make_async_remote_copy(
            src_ref=src, dst_ref=dst, send_sem=send, recv_sem=recv, device_id=to,
            device_id_type=MESH,
        )

    sib = dev(c=1 - c)
    ws = (wk, wv, wq)

    def cols(i):
        return pl.ds(pl.multiple_of(i * 256, 256), 256)

    def group(i):
        return pl.ds(pl.multiple_of(i * 128, 128), 128)

    slots = pl.ds(pl.multiple_of(y * 64 + c * 32, 32), 32)
    local = [
        pltpu.make_async_copy(tok, tokb.at[z, group(x)], loc.at[0]),
        pltpu.make_async_copy(sq.at[:, cols(x)], sqb, loc.at[1]),
        pltpu.make_async_copy(mem.at[slots, cols(x)], memb, loc.at[2]),
    ]
    last = [
        pltpu.make_async_copy(gain.at[:, cols(x)], gainb, loc.at[11]),
        pltpu.make_async_copy(dl, dlb, loc.at[12]),
    ]
    for m in range(3):
        local.append(
            pltpu.make_async_copy(ws[m].at[:, cols(x)], wb.at[m, y, x, c], loc.at[3 + m])
        )
    for cp in local + last:
        cp.start()

    barrier = pltpu.get_barrier_semaphore()

    def greet(p):
        pl.semaphore_signal(barrier, inc=1, device_id=p, device_id_type=MESH)

    greet(sib)
    for d in range(1, 4):
        greet(dev(x=xs[d]))
        greet(dev(y=ys[d]))
    pl.when(z < 3)(lambda: greet(dev(z=z + 1)))
    pl.when(z > 0)(lambda: greet(dev(z=z - 1)))
    pl.semaphore_wait(barrier, 9 - z // 3 - (3 - z) // 3)

    sent = []

    def go(cp):
        cp.start()
        sent.append(cp)

    first = 1 + z % 2
    third = 3 * (1 - z // 2)
    second = 6 - z - first - third
    order = [z, first, second, third]
    onward = [None, 3 * (z // 2), 3 - z, 3 * (z // 2)]
    middle = (z + 1) // 2 == 1

    def chain(i, src_of, send, recv):
        if i == 0:
            ref = src_of(z)
            up = remote(ref, ref, send.at[0], recv.at[z], dev(z=z + 1))
            down = remote(ref, ref, send.at[1], recv.at[z], dev(z=z - 1))
            return [(z < 3, up), (z > 0, down)]
        zi = order[i]
        ref = src_of(zi)
        return [(middle, remote(ref, ref, send.at[i + 1], recv.at[zi], dev(z=onward[i])))]

    def start_chain(*args):
        for cond, cp in chain(*args):
            pl.when(cond)(cp.start)

    def finish_chain(*args):
        for cond, cp in chain(*args):
            pl.when(cond)(cp.wait_send)

    def wait_chain(i, src_of, send, recv):
        ref = src_of(order[i])
        remote(ref, ref, send.at[0], recv.at[order[i]], sib).wait_recv()

    def half_rows(xi, h):
        return pl.ds(pl.multiple_of(xi * 128 + 64 * h, 64), 64)

    A = [(lambda zi, h=h: tokb.at[zi, half_rows(x, h)], z_s.at[h], z_r.at[h]) for h in (0, 1)]
    B = [(lambda zi, h=h: tokb.at[zi, half_rows(xs[2], h)], zb_s.at[h], zb_r.at[h]) for h in (0, 1)]

    def send_w(m):
        for d in (2, 1, 3):
            go(remote(ws[m].at[:, cols(xs[d])], wb.at[m, y, x, c], xw_s.at[m, d], xw_r.at[m, x],
                      dev(x=xs[d])))

    def send_x(i, h, k):
        zi = order[i]
        ref = tokb.at[zi, half_rows(x, h)]
        go(remote(ref, ref, xa_s.at[i, h, k], xa_r.at[zi, h, k], dev(x=xs[1 + 2 * k])))

    def wait_x(i, h, k):
        zi = order[i]
        ref = tokb.at[zi, half_rows(xs[3 - 2 * k], h)]
        remote(ref, ref, xa_s.at[0, 0, 0], xa_r.at[zi, h, k], sib).wait_recv()

    def wait_block(i):
        for h in (0, 1):
            for k in (0, 1):
                if i or h == k:
                    wait_x(i, h, k)

    def send_y(m, dx, src):
        for d in (2, 1, 3):
            go(remote(src, wb.at[m, y, xs[dx], c], yw_s.at[m, d, dx], yw_r.at[m, y, xs[dx]],
                      dev(y=ys[d])))

    def spread_own(m):
        send_y(m, 0, ws[m].at[:, cols(x)])

    def spread_w(m):
        for d in (1, 3, 2):
            ref = wb.at[m, y, xs[d], c]
            remote(ref, ref, xw_s.at[m, d], xw_r.at[m, xs[d]], sib).wait_recv()
            send_y(m, d, ref)
        local[3 + m].wait()
        ref = wb.at[m, y, :, c]
        go(remote(ref, ref, cw_s.at[m, 0], cw_r.at[m, y], sib))

    def pass_w(m):
        for d in (1, 3, 2):
            for dx in range(4):
                ref = wb.at[m, ys[d], xs[dx], c]
                remote(ref, ref, yw_s.at[m, d, dx], yw_r.at[m, ys[d], xs[dx]], sib).wait_recv()
            ref = wb.at[m, ys[d], :, c]
            go(remote(ref, ref, cw_s.at[m, d], cw_r.at[m, ys[d]], sib))

    def wait_w(m):
        for d in range(4):
            ref = wb.at[m, ys[d], :, 1 - c]
            remote(ref, ref, cw_s.at[m, d], cw_r.at[m, ys[d]], sib).wait_recv()

    def project(m, zi, fresh):
        w = wb[m, zi].reshape(1024, 256)
        r = jnp.dot(tokb[zi], w, preferred_element_type=F32)
        if fresh:
            acc[m] = r
        else:
            acc[m] += r

    def link(i, h, which):
        wait_chain(i, *which[h])
        start_chain(i, *which[h])

    def forward(h):
        ref = tokb.at[z, half_rows(xs[1 + 2 * h], h)]
        go(remote(ref, ref, f_s.at[h], f_r.at[h], dev(x=xs[3 - 2 * h])))

    def far(h):
        ref = tokb.at[z, half_rows(xs[2], h)]
        remote(ref, ref, f_s.at[h], f_r.at[h], sib).wait_recv()
        start_chain(0, *B[h])

    local[0].wait()
    start_chain(0, *A[0])
    send_x(0, 0, 1)
    send_x(0, 1, 0)
    spread_own(0)
    send_w(0)
    start_chain(0, *A[1])
    send_x(0, 1, 1)
    send_x(0, 0, 0)
    send_w(1)
    spread_own(1)
    wait_x(0, 0, 1)
    forward(0)
    wait_x(0, 1, 0)
    forward(1)
    spread_w(0)
    for h in (0, 1):
        link(1, h, A)
        send_x(1, h, 0)
        send_x(1, h, 1)
    far(0)
    far(1)
    spread_w(1)
    spread_own(2)
    send_w(2)
    for h in (0, 1):
        link(2, h, A)
        send_x(2, h, 0)
        send_x(2, h, 1)
    link(1, 0, B)
    link(1, 1, B)
    for h in (0, 1):
        link(3, h, A)
        send_x(3, h, 0)
        send_x(3, h, 1)
    pass_w(0)
    spread_w(2)
    link(2, 0, B)
    link(2, 1, B)
    pass_w(1)
    wait_block(0)
    wait_w(0)
    wait_w(1)
    project(0, z, True)
    project(1, z, True)
    wait_block(1)
    project(0, first, False)
    project(1, first, False)
    link(3, 0, B)
    link(3, 1, B)
    wait_block(2)
    project(0, second, False)
    project(1, second, False)
    wait_block(3)
    project(0, third, False)
    project(1, third, False)

    local[1].wait()
    local[2].wait()
    for cp in last:
        cp.wait()
    length = dlb[0]
    j = lax.broadcasted_iota(jnp.int32, (1, 512), 1)
    valid = y * 1024 + (j // 128) * 256 + c * 128 + j % 128 < length
    stats = []
    for h in range(2):
        hc = slice(h * 128, (h + 1) * 128)
        k = acc[0, :, hc].astype(BF16)
        v = acc[1, :, hc].astype(BF16)
        s = lax.dot_general(sqb[:, hc], k, NT, preferred_element_type=F32) * SCALING
        s = jnp.where(valid, s, NEGATIVE)
        top = jnp.max(s, axis=1, keepdims=True)
        p = jnp.where(valid, jnp.exp(s - top), 0.0)
        total = jnp.sum(p, axis=1, keepdims=True)
        high = p.astype(BF16)
        low = (p - high.astype(F32)).astype(BF16)
        a = jnp.dot(high, v, preferred_element_type=F32) + jnp.dot(
            low, v, preferred_element_type=F32
        )
        for yy in range(4):
            for cc in range(2):
                r = yy * 64 + cc * 32
                pm[cc, yy, :, hc] = a[r : r + 32]
        stats.append((top, total))
    lanes = stat_lanes(stats, 256)
    for yy in range(4):
        for cc in range(2):
            r = yy * 64 + cc * 32
            pm[cc, yy, :, 256:384] = lanes[r : r + 32]

    cp = remote(pm.at[1 - c], pr, p1.at[0], p1.at[1], sib)
    go(cp)
    cp.wait_recv()
    outs, stats = merge([pm[c].reshape(128, 384), pr[...].reshape(128, 384)])
    mg[:, :, 0:128] = outs[0].reshape(4, 32, 128)
    mg[:, :, 128:256] = outs[1].reshape(4, 32, 128)
    mg[:, :, 256:384] = stat_lanes(stats, 128).reshape(4, 32, 128)
    for d in (2, 1, 3):
        go(remote(mg.at[ys[d]], mr.at[y], p2_s.at[d], p2_r.at[y], dev(y=ys[d])))

    pass_w(2)
    wait_w(2)
    for i in range(4):
        project(2, i, i == 0)

    for d in range(1, 4):
        remote(mr.at[ys[d]], mr.at[ys[d]], p2_s.at[d], p2_r.at[ys[d]], sib).wait_recv()
    outs, stats = merge([mg[y]] + [mr[ys[d]] for d in range(1, 4)])
    packed = jnp.concatenate([outs[h] / stats[h][1] for h in range(2)], axis=1)
    combined = memb[...].astype(F32) + packed
    stacked = jnp.concatenate([combined, combined * combined, jnp.zeros((64, 256), F32)], axis=0)
    sums = lax.dot_general(
        jnp.ones((8, 256), F32), stacked, NT, precision=lax.Precision.HIGHEST,
        preferred_element_type=F32,
    )
    st[x, z] = sums
    for dz in (2, 3, 1, 0):
        for dx in (2, 1, 3, 0):
            if dx or dz:
                go(remote(st.at[x, z], st.at[x, z], p3_s.at[dx, dz], p3_r.at[x, z],
                          dev(x=xs[dx], z=zs[dz])))
    for dz in range(4):
        for dx in range(4):
            if dx or dz:
                ref = st.at[xs[dx], zs[dz]]
                remote(ref, ref, p3_s.at[dx, dz], p3_r.at[xs[dx], zs[dz]], sib).wait_recv()
    sums = jnp.sum(st[...].reshape(16, 8, 128), axis=0)
    column = jnp.transpose(sums)[:, 0:1] / D
    mean = column[0:32]
    square = column[32:64]
    inverse = lax.rsqrt(square - mean * mean + EPSILON)
    nmf[x, slots] = ((combined - mean) * inverse * gainb[...]).astype(BF16)
    ref = nmf.at[x, slots]
    for d in (2, 1, 3):
        for cc in (0, 1):
            to = dev(y=ys[d], c=(c + cc) % 2)
            go(remote(ref, ref, p4_s.at[d, cc], p4_r.at[y, c], to))
    go(remote(ref, ref, p4_s.at[0, 1], p4_r.at[y, c], sib))

    for d in range(4):
        for cc in range(2):
            if d or cc:
                c2 = (c + cc) % 2
                ref = nmf.at[x, pl.ds(pl.multiple_of(ys[d] * 64 + c2 * 32, 32), 32)]
                remote(ref, ref, p4_s.at[d, cc], p4_r.at[ys[d], c2], sib).wait_recv()

    rows = pl.ds(pl.multiple_of(c * 128, 128), 128)
    ref = nmf.at[x, rows]
    for d in (2, 1, 3):
        go(remote(ref, ref, n_s.at[d], n_r.at[x], dev(x=xs[d])))

    r = lax.broadcasted_iota(jnp.int32, (128, 1), 0)
    final = []
    for d in (2, 1, 3, 0):
        g = xs[d]
        live = y * 1024 + g * 256 + c * 128 + r < length
        for h in range(2):
            hc = slice(h * 128, (h + 1) * 128)
            q = acc[2, group(g), hc].astype(BF16)
            n = nmf[x, :, hc]
            s = lax.dot_general(q, n, NT, preferred_element_type=F32) * SCALING
            e = jnp.exp(s - jnp.max(s, axis=1, keepdims=True))
            probs = (e / jnp.sum(e, axis=1, keepdims=True)).astype(BF16)
            o = jnp.dot(probs, n, preferred_element_type=F32)
            ob[g, :, hc] = jnp.where(live, o, 0.0).astype(BF16)
        if d:
            go(remote(ob.at[g], o_un.at[:, cols(x)], u_s.at[d], u_r.at[x], dev(x=g)))
        else:
            cp = pltpu.make_async_copy(ob.at[g], o_un.at[:, cols(x)], loc.at[6])
            cp.start()
            final.append(cp)

    for d in (1, 3, 2):
        ref = nmf.at[xs[d], rows]
        remote(ref, ref, n_s.at[d], n_r.at[xs[d]], sib).wait_recv()
        go(remote(ref, ref, nc_s.at[d], nc_r.at[xs[d]], sib))
    for d in (0, 1, 3, 2):
        if d:
            ref = nmf.at[xs[d], pl.ds(pl.multiple_of((1 - c) * 128, 128), 128)]
            remote(ref, ref, nc_s.at[d], nc_r.at[xs[d]], sib).wait_recv()
        cp = pltpu.make_async_copy(nmf.at[xs[d]], o_nm.at[:, cols(xs[d])], loc.at[7 + d])
        cp.start()
        final.append(cp)
    for d in range(1, 4):
        ref = o_un.at[:, cols(xs[d])]
        remote(ref, ref, u_s.at[d], u_r.at[xs[d]], sib).wait_recv()
    for cp in final:
        cp.wait()
    for cp in sent:
        cp.wait_send()
    for i in range(4):
        for h in (0, 1):
            finish_chain(i, *A[h])
            finish_chain(i, *B[h])


def on_device(tokens, w_key, w_value, w_query, slot_queries, memory, norm_gain, doc_length):
    dma = pltpu.SemaphoreType.DMA
    anywhere = pl.BlockSpec(memory_space=pltpu.HBM)
    return pl.pallas_call(
        kernel,
        out_shape=(
            jax.ShapeDtypeStruct((128, 1024), BF16),
            jax.ShapeDtypeStruct((256, 1024), BF16),
        ),
        in_specs=[anywhere] * 8,
        out_specs=(pl.BlockSpec(memory_space=pl.ANY),) * 2,
        scratch_shapes=[
            pltpu.VMEM((4, 512, 1024), BF16),
            pltpu.VMEM((3, 4, 4, 2, 128, 256), BF16),
            pltpu.VMEM((256, 256), BF16),
            pltpu.VMEM((32, 256), BF16),
            pltpu.VMEM((1, 256), F32),
            pltpu.SMEM((1,), jnp.int32),
            pltpu.VMEM((3, 512, 256), F32),
            pltpu.VMEM((2, 4, 32, 384), F32),
            pltpu.VMEM((4, 32, 384), F32),
            pltpu.VMEM((4, 32, 384), F32),
            pltpu.VMEM((4, 32, 384), F32),
            pltpu.VMEM((4, 4, 8, 128), F32),
            pltpu.VMEM((4, 256, 256), BF16),
            pltpu.VMEM((4, 128, 256), BF16),
            dma((13,)),
            dma((2, 5)),
            dma((2, 4)),
            dma((2, 5)),
            dma((2, 4)),
            dma((4, 2, 2)),
            dma((4, 2, 2)),
            dma((2,)),
            dma((2,)),
            dma((3, 4)),
            dma((3, 4)),
            dma((3, 4, 4)),
            dma((3, 4, 4)),
            dma((3, 4)),
            dma((3, 4)),
            dma((2,)),
            dma((4,)),
            dma((4,)),
            dma((4, 4)),
            dma((4, 4)),
            dma((4, 2)),
            dma((4, 2)),
            dma((4,)),
            dma((4,)),
            dma((4,)),
            dma((4,)),
            dma((4,)),
            dma((4,)),
        ],
        compiler_params=pltpu.CompilerParams(
            collective_id=0, has_side_effects=True, vmem_limit_bytes=60 * 2**20
        ),
        name="luna",
    )(
        tokens, w_key, w_value, w_query, slot_queries, memory, norm_gain.reshape(1, 1024),
        doc_length,
    )


def solution(mesh):
    in_specs = (
        P(("dp", "seq"), "head"),
        P("seq", "head"),
        P("seq", "head"),
        P("seq", "head"),
        P("dp", "head"),
        P("dp", "head"),
        P("head"),
        P("dp"),
    )
    out_specs = (P(("dp", "seq"), "head"), P("dp", "head"))
    return jax.shard_map(
        on_device, mesh=mesh, in_specs=in_specs, out_specs=out_specs, check_vma=False
    )
```

```python
import math

import jax
import jax.numpy as jnp
from jax import lax
from jax.experimental import pallas as pl
from jax.experimental.pallas import tpu as pltpu
from jax.sharding import PartitionSpec as P

D = 4096
HEAD_DIM = 128
NEGATIVE = -1e30
EPSILON = 1e-05
SCALING = 1.0 / math.sqrt(HEAD_DIM)
MESH = pl.DeviceIdType.MESH
F32 = jnp.float32
BF16 = jnp.bfloat16
NT = (((1,), (1,)), ((), ()))


def merge(pieces):
    outs, stats = [], []
    for h in range(2):
        tops = [p[:, 256 + 2 * h : 257 + 2 * h] for p in pieces]
        sums = [p[:, 257 + 2 * h : 258 + 2 * h] for p in pieces]
        accs = [p[:, h * 128 : (h + 1) * 128] for p in pieces]
        top = tops[0]
        for t in tops[1:]:
            top = jnp.maximum(top, t)
        factors = [jnp.exp(t - top) for t in tops]
        total = sum(s * f for s, f in zip(sums, factors))
        acc = sum(a * f for a, f in zip(accs, factors))
        outs.append(acc)
        stats.append((top, total))
    return outs, stats


def stat_lanes(stats, rows):
    lane = lax.broadcasted_iota(jnp.int32, (rows, 128), 1)
    (m0, s0), (m1, s1) = stats
    return jnp.where(lane == 0, m0, jnp.where(lane == 1, s0, jnp.where(lane == 2, m1, s1)))


def kernel(
    tok, wk, wv, wq, sq, mem, gain, dl,
    o_un, o_nm,
    tokb, wb, sqb, memb, gainb, dlb, acc, pm, pr, mg, mr, st, nmf, nx, ob,
    loc, z_s, z_r, zb_s, zb_r, xa_s, xa_r, f_s, f_r, xw_s, xw_r, yw_s, yw_r, cw_s, cw_r,
    p1, p2_s, p2_r, p3_s, p3_r, p4_s, p4_r, n_s, n_r, m_s, m_r, nc_s, nc_r, u_s, u_r,
):
    seq = lax.axis_index("seq")
    z = lax.axis_index("head")
    dp = lax.axis_index("dp")
    y, x, c = seq // 8, (seq // 2) % 4, seq % 2
    xs = [(x + d) % 4 for d in range(4)]
    ys = [(y + d) % 4 for d in range(4)]
    zs = [(z + d) % 4 for d in range(4)]

    def dev(x=x, y=y, z=z, c=c):
        return (y * 8 + x * 2 + c, z, dp)

    def remote(src, dst, send, recv, to):
        return pltpu.make_async_remote_copy(
            src_ref=src, dst_ref=dst, send_sem=send, recv_sem=recv, device_id=to,
            device_id_type=MESH,
        )

    sib = dev(c=1 - c)
    ws = (wk, wv, wq)

    def cols(i):
        return pl.ds(pl.multiple_of(i * 256, 256), 256)

    def group(i):
        return pl.ds(pl.multiple_of(i * 128, 128), 128)

    slots = pl.ds(pl.multiple_of(y * 64 + c * 32, 32), 32)
    local = [
        pltpu.make_async_copy(tok, tokb.at[z, group(x)], loc.at[0]),
        pltpu.make_async_copy(sq.at[:, cols(x)], sqb, loc.at[1]),
        pltpu.make_async_copy(mem.at[slots, cols(x)], memb, loc.at[2]),
    ]
    last = [
        pltpu.make_async_copy(gain.at[:, cols(x)], gainb, loc.at[11]),
        pltpu.make_async_copy(dl, dlb, loc.at[12]),
    ]
    for m in range(3):
        local.append(
            pltpu.make_async_copy(ws[m].at[:, cols(x)], wb.at[m, y, x, c], loc.at[3 + m])
        )
    for cp in local + last:
        cp.start()

    barrier = pltpu.get_barrier_semaphore()

    def greet(p):
        pl.semaphore_signal(barrier, inc=1, device_id=p, device_id_type=MESH)

    greet(sib)
    for d in range(1, 4):
        greet(dev(x=xs[d]))
        greet(dev(y=ys[d]))
    pl.when(z < 3)(lambda: greet(dev(z=z + 1)))
    pl.when(z > 0)(lambda: greet(dev(z=z - 1)))
    pl.semaphore_wait(barrier, 9 - z // 3 - (3 - z) // 3)

    sent = []

    def go(cp):
        cp.start()
        sent.append(cp)

    first = 1 + z % 2
    third = 3 * (1 - z // 2)
    second = 6 - z - first - third
    order = [z, first, second, third]
    onward = [None, 3 * (z // 2), 3 - z, 3 * (z // 2)]
    middle = (z + 1) // 2 == 1

    def chain(i, src_of, send, recv):
        if i == 0:
            ref = src_of(z)
            up = remote(ref, ref, send.at[0], recv.at[z], dev(z=z + 1))
            down = remote(ref, ref, send.at[1], recv.at[z], dev(z=z - 1))
            return [(z < 3, up), (z > 0, down)]
        zi = order[i]
        ref = src_of(zi)
        return [(middle, remote(ref, ref, send.at[i + 1], recv.at[zi], dev(z=onward[i])))]

    def start_chain(*args):
        for cond, cp in chain(*args):
            pl.when(cond)(cp.start)

    def finish_chain(*args):
        for cond, cp in chain(*args):
            pl.when(cond)(cp.wait_send)

    def wait_chain(i, src_of, send, recv):
        ref = src_of(order[i])
        remote(ref, ref, send.at[0], recv.at[order[i]], sib).wait_recv()

    def half_rows(xi, h):
        return pl.ds(pl.multiple_of(xi * 128 + 64 * h, 64), 64)

    A = [(lambda zi, h=h: tokb.at[zi, half_rows(x, h)], z_s.at[h], z_r.at[h]) for h in (0, 1)]
    B = [(lambda zi, h=h: tokb.at[zi, half_rows(xs[2], h)], zb_s.at[h], zb_r.at[h]) for h in (0, 1)]

    def send_w(m):
        for d in (2, 1, 3):
            go(remote(ws[m].at[:, cols(xs[d])], wb.at[m, y, x, c], xw_s.at[m, d], xw_r.at[m, x],
                      dev(x=xs[d])))

    def send_x(i, h, k):
        zi = order[i]
        ref = tokb.at[zi, half_rows(x, h)]
        go(remote(ref, ref, xa_s.at[i, h, k], xa_r.at[zi, h, k], dev(x=xs[1 + 2 * k])))

    def wait_x(i, h, k):
        zi = order[i]
        ref = tokb.at[zi, half_rows(xs[3 - 2 * k], h)]
        remote(ref, ref, xa_s.at[0, 0, 0], xa_r.at[zi, h, k], sib).wait_recv()

    def wait_block(i):
        for h in (0, 1):
            for k in (0, 1):
                if i or h == k:
                    wait_x(i, h, k)

    def send_y(m, dx, src):
        for d in (2, 1, 3):
            go(remote(src, wb.at[m, y, xs[dx], c], yw_s.at[m, d, dx], yw_r.at[m, y, xs[dx]],
                      dev(y=ys[d])))

    def spread_own(m):
        send_y(m, 0, ws[m].at[:, cols(x)])

    def spread_w(m):
        for d in (1, 3, 2):
            ref = wb.at[m, y, xs[d], c]
            remote(ref, ref, xw_s.at[m, d], xw_r.at[m, xs[d]], sib).wait_recv()
            send_y(m, d, ref)
        local[3 + m].wait()
        ref = wb.at[m, y, :, c]
        go(remote(ref, ref, cw_s.at[m, 0], cw_r.at[m, y], sib))

    def pass_w(m):
        for d in (1, 3, 2):
            for dx in range(4):
                ref = wb.at[m, ys[d], xs[dx], c]
                remote(ref, ref, yw_s.at[m, d, dx], yw_r.at[m, ys[d], xs[dx]], sib).wait_recv()
            ref = wb.at[m, ys[d], :, c]
            go(remote(ref, ref, cw_s.at[m, d], cw_r.at[m, ys[d]], sib))

    def wait_w(m):
        for d in range(4):
            ref = wb.at[m, ys[d], :, 1 - c]
            remote(ref, ref, cw_s.at[m, d], cw_r.at[m, ys[d]], sib).wait_recv()

    def project(m, zi, fresh):
        w = wb[m, zi].reshape(1024, 256)
        r = jnp.dot(tokb[zi], w, preferred_element_type=F32)
        if fresh:
            acc[m] = r
        else:
            acc[m] += r

    def link(i, h, which):
        wait_chain(i, *which[h])
        start_chain(i, *which[h])

    def forward(h):
        ref = tokb.at[z, half_rows(xs[1 + 2 * h], h)]
        go(remote(ref, ref, f_s.at[h], f_r.at[h], dev(x=xs[3 - 2 * h])))

    def far(h):
        ref = tokb.at[z, half_rows(xs[2], h)]
        remote(ref, ref, f_s.at[h], f_r.at[h], sib).wait_recv()
        start_chain(0, *B[h])

    def pass_block(i):
        for h in (0, 1):
            link(i, h, A)
            send_x(i, h, 0)
            send_x(i, h, 1)

    def pass_far(i):
        for h in (0, 1):
            link(i, h, B)

    local[0].wait()
    start_chain(0, *A[0])
    send_x(0, 0, 1)
    send_x(0, 1, 0)
    spread_own(0)
    start_chain(0, *A[1])
    send_x(0, 1, 1)
    send_x(0, 0, 0)
    spread_own(1)
    wait_x(0, 0, 1)
    forward(0)
    wait_x(0, 1, 0)
    forward(1)
    send_w(0)
    pass_block(1)
    send_w(1)
    far(0)
    far(1)
    spread_w(0)
    pass_block(2)
    pass_far(1)
    spread_w(1)
    pass_block(3)
    send_w(2)
    spread_own(2)
    pass_w(0)
    pass_far(2)
    pass_w(1)
    pass_far(3)
    spread_w(2)
    wait_w(0)
    wait_w(1)
    for i, zi in enumerate(order):
        wait_block(i)
        project(0, zi, i == 0)
        project(1, zi, i == 0)

    local[1].wait()
    local[2].wait()
    for cp in last:
        cp.wait()
    length = dlb[0]
    j = lax.broadcasted_iota(jnp.int32, (1, 512), 1)
    valid = y * 1024 + (j // 128) * 256 + c * 128 + j % 128 < length
    stats = []
    for h in range(2):
        hc = slice(h * 128, (h + 1) * 128)
        k = acc[0, :, hc].astype(BF16)
        v = acc[1, :, hc].astype(BF16)
        s = lax.dot_general(sqb[:, hc], k, NT, preferred_element_type=F32) * SCALING
        s = jnp.where(valid, s, NEGATIVE)
        top = jnp.max(s, axis=1, keepdims=True)
        p = jnp.where(valid, jnp.exp(s - top), 0.0)
        total = jnp.sum(p, axis=1, keepdims=True)
        high = p.astype(BF16)
        low = (p - high.astype(F32)).astype(BF16)
        a = jnp.dot(high, v, preferred_element_type=F32) + jnp.dot(
            low, v, preferred_element_type=F32
        )
        for yy in range(4):
            for cc in range(2):
                r = yy * 64 + cc * 32
                pm[cc, yy, :, hc] = a[r : r + 32]
        stats.append((top, total))
    lanes = stat_lanes(stats, 256)
    for yy in range(4):
        for cc in range(2):
            r = yy * 64 + cc * 32
            pm[cc, yy, :, 256:384] = lanes[r : r + 32]

    cp = remote(pm.at[1 - c], pr, p1.at[0], p1.at[1], sib)
    go(cp)
    cp.wait_recv()
    outs, stats = merge([pm[c].reshape(128, 384), pr[...].reshape(128, 384)])
    mg[:, :, 0:128] = outs[0].reshape(4, 32, 128)
    mg[:, :, 128:256] = outs[1].reshape(4, 32, 128)
    mg[:, :, 256:384] = stat_lanes(stats, 128).reshape(4, 32, 128)
    for d in (2, 1, 3):
        go(remote(mg.at[ys[d]], mr.at[y], p2_s.at[d], p2_r.at[y], dev(y=ys[d])))

    for d in range(1, 4):
        remote(mr.at[ys[d]], mr.at[ys[d]], p2_s.at[d], p2_r.at[ys[d]], sib).wait_recv()
    outs, stats = merge([mg[y]] + [mr[ys[d]] for d in range(1, 4)])
    packed = jnp.concatenate([outs[h] / stats[h][1] for h in range(2)], axis=1)
    combined = memb[...].astype(F32) + packed
    stacked = jnp.concatenate([combined, combined * combined, jnp.zeros((64, 256), F32)], axis=0)
    sums = lax.dot_general(
        jnp.ones((8, 256), F32), stacked, NT, precision=lax.Precision.HIGHEST,
        preferred_element_type=F32,
    )
    st[x, z] = sums
    early = list(sent)
    sent.clear()
    for dz in (2, 3, 1, 0):
        for dx in (2, 1, 3, 0):
            if dx or dz:
                go(remote(st.at[x, z], st.at[x, z], p3_s.at[dx, dz], p3_r.at[x, z],
                          dev(x=xs[dx], z=zs[dz])))
    for dz in range(4):
        for dx in range(4):
            if dx or dz:
                ref = st.at[xs[dx], zs[dz]]
                remote(ref, ref, p3_s.at[dx, dz], p3_r.at[xs[dx], zs[dz]], sib).wait_recv()
    sums = jnp.sum(st[...].reshape(16, 8, 128), axis=0)
    column = jnp.transpose(sums)[:, 0:1] / D
    mean = column[0:32]
    square = column[32:64]
    inverse = lax.rsqrt(square - mean * mean + EPSILON)
    piece = ((combined - mean) * inverse * gainb[...]).astype(BF16)
    nmf[slots] = piece
    nx[:, cols(x)] = piece
    ref = nmf.at[slots]
    for d in (2, 1, 3):
        for cc in (0, 1):
            to = dev(y=ys[d], c=(c + cc) % 2)
            go(remote(ref, ref, p4_s.at[d, cc], p4_r.at[y, c], to))
    go(remote(ref, ref, p4_s.at[0, 1], p4_r.at[y, c], sib))
    for d in (2, 1, 3):
        go(remote(ref, nx.at[:, cols(x)], n_s.at[d], n_r.at[x], dev(x=xs[d])))

    pass_w(2)
    wait_w(2)
    for i in range(4):
        project(2, i, i == 0)
    for cp in early:
        cp.wait_send()
    for i in range(4):
        for h in (0, 1):
            finish_chain(i, *A[h])
            finish_chain(i, *B[h])

    for d in range(4):
        for cc in range(2):
            if d or cc:
                c2 = (c + cc) % 2
                ref = nmf.at[pl.ds(pl.multiple_of(ys[d] * 64 + c2 * 32, 32), 32)]
                remote(ref, ref, p4_s.at[d, cc], p4_r.at[ys[d], c2], sib).wait_recv()

    for d in range(1, 4):
        ref = nx.at[:, cols(xs[d])]
        remote(ref, ref, n_s.at[d], n_r.at[xs[d]], sib).wait_recv()
    final = [pltpu.make_async_copy(nx, o_nm.at[slots], loc.at[7])]
    final[0].start()
    for d in (2, 1, 3):
        go(remote(nx, o_nm.at[slots], m_s.at[d], m_r.at[y], dev(y=ys[d])))
    go(remote(nx, o_nm.at[slots], nc_s.at[0], nc_r.at[y], sib))

    r = lax.broadcasted_iota(jnp.int32, (128, 1), 0)
    for d in (2, 1, 3, 0):
        g = xs[d]
        live = y * 1024 + g * 256 + c * 128 + r < length
        for h in range(2):
            hc = slice(h * 128, (h + 1) * 128)
            q = acc[2, group(g), hc].astype(BF16)
            n = nmf[:, hc]
            s = lax.dot_general(q, n, NT, preferred_element_type=F32) * SCALING
            e = jnp.exp(s - jnp.max(s, axis=1, keepdims=True))
            probs = (e / jnp.sum(e, axis=1, keepdims=True)).astype(BF16)
            o = jnp.dot(probs, n, preferred_element_type=F32)
            ob[g, :, hc] = jnp.where(live, o, 0.0).astype(BF16)
        if d:
            go(remote(ob.at[g], o_un.at[:, cols(x)], u_s.at[d], u_r.at[x], dev(x=g)))
        else:
            cp = pltpu.make_async_copy(ob.at[g], o_un.at[:, cols(x)], loc.at[6])
            cp.start()
            final.append(cp)

    def rows_of(yi, ci):
        return o_nm.at[pl.ds(pl.multiple_of(yi * 64 + ci * 32, 32), 32)]

    for d in (1, 3, 2):
        ref = rows_of(ys[d], c)
        remote(ref, ref, m_s.at[d], m_r.at[ys[d]], sib).wait_recv()
        go(remote(ref, ref, nc_s.at[d], nc_r.at[ys[d]], sib))
    for d in range(1, 4):
        ref = o_un.at[:, cols(xs[d])]
        remote(ref, ref, u_s.at[d], u_r.at[xs[d]], sib).wait_recv()
    for d in range(4):
        ref = rows_of(ys[d], 1 - c)
        remote(ref, ref, nc_s.at[d], nc_r.at[ys[d]], sib).wait_recv()
    for cp in final:
        cp.wait()
    for cp in sent:
        cp.wait_send()


def on_device(tokens, w_key, w_value, w_query, slot_queries, memory, norm_gain, doc_length):
    dma = pltpu.SemaphoreType.DMA
    anywhere = pl.BlockSpec(memory_space=pltpu.HBM)
    return pl.pallas_call(
        kernel,
        out_shape=(
            pltpu.VMEM((128, 1024), BF16),
            pltpu.VMEM((256, 1024), BF16),
        ),
        in_specs=[anywhere] * 8,
        out_specs=(pl.BlockSpec(memory_space=pl.ANY),) * 2,
        scratch_shapes=[
            pltpu.VMEM((4, 512, 1024), BF16),
            pltpu.VMEM((3, 4, 4, 2, 128, 256), BF16),
            pltpu.VMEM((256, 256), BF16),
            pltpu.VMEM((32, 256), BF16),
            pltpu.VMEM((1, 256), F32),
            pltpu.SMEM((1,), jnp.int32),
            pltpu.VMEM((3, 512, 256), F32),
            pltpu.VMEM((2, 4, 32, 384), F32),
            pltpu.VMEM((4, 32, 384), F32),
            pltpu.VMEM((4, 32, 384), F32),
            pltpu.VMEM((4, 32, 384), F32),
            pltpu.VMEM((4, 4, 8, 128), F32),
            pltpu.VMEM((256, 256), BF16),
            pltpu.VMEM((32, 1024), BF16),
            pltpu.VMEM((4, 128, 256), BF16),
            dma((13,)),
            dma((2, 5)),
            dma((2, 4)),
            dma((2, 5)),
            dma((2, 4)),
            dma((4, 2, 2)),
            dma((4, 2, 2)),
            dma((2,)),
            dma((2,)),
            dma((3, 4)),
            dma((3, 4)),
            dma((3, 4, 4)),
            dma((3, 4, 4)),
            dma((3, 4)),
            dma((3, 4)),
            dma((2,)),
            dma((4,)),
            dma((4,)),
            dma((4, 4)),
            dma((4, 4)),
            dma((4, 2)),
            dma((4, 2)),
            dma((4,)),
            dma((4,)),
            dma((4,)),
            dma((4,)),
            dma((4,)),
            dma((4,)),
            dma((4,)),
            dma((4,)),
        ],
        compiler_params=pltpu.CompilerParams(
            collective_id=0, has_side_effects=True, vmem_limit_bytes=60 * 2**20
        ),
        name="luna",
    )(
        tokens, w_key, w_value, w_query, slot_queries, memory, norm_gain.reshape(1, 1024),
        doc_length,
    )


def solution(mesh):
    in_specs = (
        P(("dp", "seq"), "head"),
        P("seq", "head"),
        P("seq", "head"),
        P("seq", "head"),
        P("dp", "head"),
        P("dp", "head"),
        P("head"),
        P("dp"),
    )
    out_specs = (P(("dp", "seq"), "head"), P("dp", "head"))
    return jax.shard_map(
        on_device, mesh=mesh, in_specs=in_specs, out_specs=out_specs, check_vma=False
    )
```

```python
import math

import jax
import jax.numpy as jnp
from jax import lax
from jax.experimental import pallas as pl
from jax.experimental.pallas import tpu as pltpu
from jax.sharding import PartitionSpec as P

D = 4096
HEAD_DIM = 128
NEGATIVE = -1e30
EPSILON = 1e-05
SCALING = 1.0 / math.sqrt(HEAD_DIM)
MESH = pl.DeviceIdType.MESH
F32 = jnp.float32
BF16 = jnp.bfloat16
NT = (((1,), (1,)), ((), ()))


def merge(pieces):
    outs, stats = [], []
    for h in range(2):
        tops = [p[:, 256 + 2 * h : 257 + 2 * h] for p in pieces]
        sums = [p[:, 257 + 2 * h : 258 + 2 * h] for p in pieces]
        accs = [p[:, h * 128 : (h + 1) * 128] for p in pieces]
        top = tops[0]
        for t in tops[1:]:
            top = jnp.maximum(top, t)
        factors = [jnp.exp(t - top) for t in tops]
        total = sum(s * f for s, f in zip(sums, factors))
        acc = sum(a * f for a, f in zip(accs, factors))
        outs.append(acc)
        stats.append((top, total))
    return outs, stats


def stat_lanes(stats, rows):
    lane = lax.broadcasted_iota(jnp.int32, (rows, 128), 1)
    (m0, s0), (m1, s1) = stats
    return jnp.where(lane == 0, m0, jnp.where(lane == 1, s0, jnp.where(lane == 2, m1, s1)))


def kernel(
    tok, wk, wv, wq, sq, mem, gain, dl,
    o_un, o_nm,
    tokb, wb, sqb, memb, gainb, dlb, acc, pm, pr, mg, mr, st, nmf, nx, ob,
    loc, z_s, z_r, zb_s, zb_r, xa_s, xa_r, f_s, f_r, xw_s, xw_r, yw_s, yw_r, cw_s, cw_r,
    p1, p2_s, p2_r, p3_s, p3_r, p4_s, p4_r, n_s, n_r, m_s, m_r, nc_s, nc_r, u_s, u_r,
):
    seq = lax.axis_index("seq")
    z = lax.axis_index("head")
    dp = lax.axis_index("dp")
    y, x, c = seq // 8, (seq // 2) % 4, seq % 2
    xs = [(x + d) % 4 for d in range(4)]
    ys = [(y + d) % 4 for d in range(4)]
    zs = [(z + d) % 4 for d in range(4)]

    def dev(x=x, y=y, z=z, c=c):
        return (y * 8 + x * 2 + c, z, dp)

    def remote(src, dst, send, recv, to):
        return pltpu.make_async_remote_copy(
            src_ref=src, dst_ref=dst, send_sem=send, recv_sem=recv, device_id=to,
            device_id_type=MESH,
        )

    sib = dev(c=1 - c)
    ws = (wk, wv, wq)

    def cols(i):
        return pl.ds(pl.multiple_of(i * 256, 256), 256)

    def group(i):
        return pl.ds(pl.multiple_of(i * 128, 128), 128)

    slots = pl.ds(pl.multiple_of(y * 64 + c * 32, 32), 32)
    local = [
        pltpu.make_async_copy(tok, tokb.at[z, group(x)], loc.at[0]),
        pltpu.make_async_copy(sq.at[:, cols(x)], sqb, loc.at[1]),
        pltpu.make_async_copy(mem.at[slots, cols(x)], memb, loc.at[2]),
    ]
    last = [
        pltpu.make_async_copy(gain.at[:, cols(x)], gainb, loc.at[11]),
        pltpu.make_async_copy(dl, dlb, loc.at[12]),
    ]
    for m in range(3):
        local.append(
            pltpu.make_async_copy(ws[m].at[:, cols(x)], wb.at[m, y, x, c], loc.at[3 + m])
        )
    for cp in local + last:
        cp.start()

    barrier = pltpu.get_barrier_semaphore()

    def greet(p):
        pl.semaphore_signal(barrier, inc=1, device_id=p, device_id_type=MESH)

    greet(sib)
    for d in range(1, 4):
        greet(dev(x=xs[d]))
        greet(dev(y=ys[d]))
    pl.when(z < 3)(lambda: greet(dev(z=z + 1)))
    pl.when(z > 0)(lambda: greet(dev(z=z - 1)))
    pl.semaphore_wait(barrier, 9 - z // 3 - (3 - z) // 3)

    sent = []

    def go(cp):
        cp.start()
        sent.append(cp)

    first = 1 + z % 2
    third = 3 * (1 - z // 2)
    second = 6 - z - first - third
    order = [z, first, second, third]
    onward = [None, 3 * (z // 2), 3 - z, 3 * (z // 2)]
    middle = (z + 1) // 2 == 1

    def chain(i, src_of, send, recv):
        if i == 0:
            ref = src_of(z)
            up = remote(ref, ref, send.at[0], recv.at[z], dev(z=z + 1))
            down = remote(ref, ref, send.at[1], recv.at[z], dev(z=z - 1))
            return [(z < 3, up), (z > 0, down)]
        zi = order[i]
        ref = src_of(zi)
        return [(middle, remote(ref, ref, send.at[i + 1], recv.at[zi], dev(z=onward[i])))]

    def start_chain(*args):
        for cond, cp in chain(*args):
            pl.when(cond)(cp.start)

    def finish_chain(*args):
        for cond, cp in chain(*args):
            pl.when(cond)(cp.wait_send)

    def wait_chain(i, src_of, send, recv):
        ref = src_of(order[i])
        remote(ref, ref, send.at[0], recv.at[order[i]], sib).wait_recv()

    def half_rows(xi, h):
        return pl.ds(pl.multiple_of(xi * 128 + 64 * h, 64), 64)

    A = [(lambda zi, h=h: tokb.at[zi, half_rows(x, h)], z_s.at[h], z_r.at[h]) for h in (0, 1)]
    B = [(lambda zi, h=h: tokb.at[zi, half_rows(xs[2], h)], zb_s.at[h], zb_r.at[h]) for h in (0, 1)]

    def send_w(m):
        for d in (2, 1, 3):
            go(remote(ws[m].at[:, cols(xs[d])], wb.at[m, y, x, c], xw_s.at[m, d], xw_r.at[m, x],
                      dev(x=xs[d])))

    def send_x(i, h, k):
        zi = order[i]
        ref = tokb.at[zi, half_rows(x, h)]
        go(remote(ref, ref, xa_s.at[i, h, k], xa_r.at[zi, h, k], dev(x=xs[1 + 2 * k])))

    def wait_x(i, h, k):
        zi = order[i]
        ref = tokb.at[zi, half_rows(xs[3 - 2 * k], h)]
        remote(ref, ref, xa_s.at[0, 0, 0], xa_r.at[zi, h, k], sib).wait_recv()

    def wait_block(i):
        for h in (0, 1):
            for k in (0, 1):
                if i or h == k:
                    wait_x(i, h, k)

    def send_y(m, dx, src):
        for d in (2, 1, 3):
            go(remote(src, wb.at[m, y, xs[dx], c], yw_s.at[m, d, dx], yw_r.at[m, y, xs[dx]],
                      dev(y=ys[d])))

    def spread_own(m):
        send_y(m, 0, ws[m].at[:, cols(x)])

    def spread_w(m):
        for d in (1, 3, 2):
            ref = wb.at[m, y, xs[d], c]
            remote(ref, ref, xw_s.at[m, d], xw_r.at[m, xs[d]], sib).wait_recv()
            send_y(m, d, ref)
        local[3 + m].wait()
        ref = wb.at[m, y, :, c]
        go(remote(ref, ref, cw_s.at[m, 0], cw_r.at[m, y], sib))

    def pass_w(m):
        for d in (1, 3, 2):
            for dx in range(4):
                ref = wb.at[m, ys[d], xs[dx], c]
                remote(ref, ref, yw_s.at[m, d, dx], yw_r.at[m, ys[d], xs[dx]], sib).wait_recv()
            ref = wb.at[m, ys[d], :, c]
            go(remote(ref, ref, cw_s.at[m, d], cw_r.at[m, ys[d]], sib))

    def wait_w(m):
        for d in range(4):
            ref = wb.at[m, ys[d], :, 1 - c]
            remote(ref, ref, cw_s.at[m, d], cw_r.at[m, ys[d]], sib).wait_recv()

    def project(m, zi, fresh):
        w = wb[m, zi].reshape(1024, 256)
        r = jnp.dot(tokb[zi], w, preferred_element_type=F32)
        if fresh:
            acc[m] = r
        else:
            acc[m] += r

    def link(i, h, which):
        wait_chain(i, *which[h])
        start_chain(i, *which[h])

    def forward(h):
        ref = tokb.at[z, half_rows(xs[1 + 2 * h], h)]
        go(remote(ref, ref, f_s.at[h], f_r.at[h], dev(x=xs[3 - 2 * h])))

    def far(h):
        ref = tokb.at[z, half_rows(xs[2], h)]
        remote(ref, ref, f_s.at[h], f_r.at[h], sib).wait_recv()
        start_chain(0, *B[h])

    def pass_block(i):
        for h in (0, 1):
            link(i, h, A)
            send_x(i, h, 0)
            send_x(i, h, 1)

    def pass_far(i):
        for h in (0, 1):
            link(i, h, B)

    local[0].wait()
    start_chain(0, *A[0])
    send_x(0, 0, 1)
    send_x(0, 1, 0)
    spread_own(0)
    start_chain(0, *A[1])
    send_x(0, 1, 1)
    send_x(0, 0, 0)
    spread_own(1)
    wait_x(0, 0, 1)
    forward(0)
    wait_x(0, 1, 0)
    forward(1)
    send_w(0)
    pass_block(1)
    send_w(1)
    spread_w(0)
    far(0)
    far(1)
    pass_block(2)
    pass_far(1)
    spread_w(1)
    pass_block(3)
    send_w(2)
    spread_own(2)
    pass_w(0)
    pass_far(2)
    pass_w(1)
    pass_far(3)
    spread_w(2)
    wait_w(0)
    wait_w(1)
    for i, zi in enumerate(order):
        wait_block(i)
        project(0, zi, i == 0)
        project(1, zi, i == 0)

    local[1].wait()
    local[2].wait()
    for cp in last:
        cp.wait()
    length = dlb[0]
    j = lax.broadcasted_iota(jnp.int32, (1, 512), 1)
    valid = y * 1024 + (j // 128) * 256 + c * 128 + j % 128 < length
    stats = []
    for h in range(2):
        hc = slice(h * 128, (h + 1) * 128)
        k = acc[0, :, hc].astype(BF16)
        v = acc[1, :, hc].astype(BF16)
        s = lax.dot_general(sqb[:, hc], k, NT, preferred_element_type=F32) * SCALING
        s = jnp.where(valid, s, NEGATIVE)
        top = jnp.max(s, axis=1, keepdims=True)
        p = jnp.where(valid, jnp.exp(s - top), 0.0)
        total = jnp.sum(p, axis=1, keepdims=True)
        high = p.astype(BF16)
        low = (p - high.astype(F32)).astype(BF16)
        a = jnp.dot(high, v, preferred_element_type=F32) + jnp.dot(
            low, v, preferred_element_type=F32
        )
        for yy in range(4):
            for cc in range(2):
                r = yy * 64 + cc * 32
                pm[cc, yy, :, hc] = a[r : r + 32]
        stats.append((top, total))
    lanes = stat_lanes(stats, 256)
    for yy in range(4):
        for cc in range(2):
            r = yy * 64 + cc * 32
            pm[cc, yy, :, 256:384] = lanes[r : r + 32]

    cp = remote(pm.at[1 - c], pr, p1.at[0], p1.at[1], sib)
    go(cp)
    cp.wait_recv()
    outs, stats = merge([pm[c].reshape(128, 384), pr[...].reshape(128, 384)])
    mg[:, :, 0:128] = outs[0].reshape(4, 32, 128)
    mg[:, :, 128:256] = outs[1].reshape(4, 32, 128)
    mg[:, :, 256:384] = stat_lanes(stats, 128).reshape(4, 32, 128)
    for d in (2, 1, 3):
        go(remote(mg.at[ys[d]], mr.at[y], p2_s.at[d], p2_r.at[y], dev(y=ys[d])))

    for d in range(1, 4):
        remote(mr.at[ys[d]], mr.at[ys[d]], p2_s.at[d], p2_r.at[ys[d]], sib).wait_recv()
    outs, stats = merge([mg[y]] + [mr[ys[d]] for d in range(1, 4)])
    packed = jnp.concatenate([outs[h] / stats[h][1] for h in range(2)], axis=1)
    combined = memb[...].astype(F32) + packed
    stacked = jnp.concatenate([combined, combined * combined, jnp.zeros((64, 256), F32)], axis=0)
    sums = lax.dot_general(
        jnp.ones((8, 256), F32), stacked, NT, precision=lax.Precision.HIGHEST,
        preferred_element_type=F32,
    )
    st[x, z] = sums
    early = list(sent)
    sent.clear()
    for dz in (2, 3, 1, 0):
        for dx in (2, 1, 3, 0):
            if dx or dz:
                go(remote(st.at[x, z], st.at[x, z], p3_s.at[dx, dz], p3_r.at[x, z],
                          dev(x=xs[dx], z=zs[dz])))
    for dz in range(4):
        for dx in range(4):
            if dx or dz:
                ref = st.at[xs[dx], zs[dz]]
                remote(ref, ref, p3_s.at[dx, dz], p3_r.at[xs[dx], zs[dz]], sib).wait_recv()
    sums = jnp.sum(st[...].reshape(16, 8, 128), axis=0)
    column = jnp.transpose(sums)[:, 0:1] / D
    mean = column[0:32]
    square = column[32:64]
    inverse = lax.rsqrt(square - mean * mean + EPSILON)
    piece = ((combined - mean) * inverse * gainb[...]).astype(BF16)
    nmf[slots] = piece
    nx[:, cols(x)] = piece
    ref = nmf.at[slots]
    for d in (2, 1, 3):
        for cc in (0, 1):
            to = dev(y=ys[d], c=(c + cc) % 2)
            go(remote(ref, ref, p4_s.at[d, cc], p4_r.at[y, c], to))
    go(remote(ref, ref, p4_s.at[0, 1], p4_r.at[y, c], sib))
    for d in (2, 1, 3):
        go(remote(ref, nx.at[:, cols(x)], n_s.at[d], n_r.at[x], dev(x=xs[d])))

    pass_w(2)
    wait_w(2)
    for i in range(4):
        project(2, i, i == 0)

    for d in range(4):
        for cc in range(2):
            if d or cc:
                c2 = (c + cc) % 2
                ref = nmf.at[pl.ds(pl.multiple_of(ys[d] * 64 + c2 * 32, 32), 32)]
                remote(ref, ref, p4_s.at[d, cc], p4_r.at[ys[d], c2], sib).wait_recv()

    for d in range(1, 4):
        ref = nx.at[:, cols(xs[d])]
        remote(ref, ref, n_s.at[d], n_r.at[xs[d]], sib).wait_recv()
    final = [pltpu.make_async_copy(nx, o_nm.at[slots], loc.at[7])]
    final[0].start()
    for d in (2, 1, 3):
        go(remote(nx, o_nm.at[slots], m_s.at[d], m_r.at[y], dev(y=ys[d])))
    go(remote(nx, o_nm.at[slots], nc_s.at[0], nc_r.at[y], sib))

    r = lax.broadcasted_iota(jnp.int32, (128, 1), 0)
    for d in (2, 1, 3, 0):
        g = xs[d]
        live = y * 1024 + g * 256 + c * 128 + r < length
        for h in range(2):
            hc = slice(h * 128, (h + 1) * 128)
            q = acc[2, group(g), hc].astype(BF16)
            n = nmf[:, hc]
            s = lax.dot_general(q, n, NT, preferred_element_type=F32) * SCALING
            e = jnp.exp(s - jnp.max(s, axis=1, keepdims=True))
            probs = (e / jnp.sum(e, axis=1, keepdims=True)).astype(BF16)
            o = jnp.dot(probs, n, preferred_element_type=F32)
            ob[g, :, hc] = jnp.where(live, o, 0.0).astype(BF16)
        if d:
            go(remote(ob.at[g], o_un.at[:, cols(x)], u_s.at[d], u_r.at[x], dev(x=g)))
        else:
            cp = pltpu.make_async_copy(ob.at[g], o_un.at[:, cols(x)], loc.at[6])
            cp.start()
            final.append(cp)

    def rows_of(yi, ci):
        return o_nm.at[pl.ds(pl.multiple_of(yi * 64 + ci * 32, 32), 32)]

    for cp in early:
        cp.wait_send()
    for i in range(4):
        for h in (0, 1):
            finish_chain(i, *A[h])
            finish_chain(i, *B[h])
    for d in (1, 3, 2):
        ref = rows_of(ys[d], c)
        remote(ref, ref, m_s.at[d], m_r.at[ys[d]], sib).wait_recv()
        go(remote(ref, ref, nc_s.at[d], nc_r.at[ys[d]], sib))
    for d in range(1, 4):
        ref = o_un.at[:, cols(xs[d])]
        remote(ref, ref, u_s.at[d], u_r.at[xs[d]], sib).wait_recv()
    for d in range(4):
        ref = rows_of(ys[d], 1 - c)
        remote(ref, ref, nc_s.at[d], nc_r.at[ys[d]], sib).wait_recv()
    for cp in final:
        cp.wait()
    for cp in sent:
        cp.wait_send()


def store(a, b, out_a, out_b, sem):
    copies = [
        pltpu.make_async_copy(a, out_a, sem.at[0]),
        pltpu.make_async_copy(b, out_b, sem.at[1]),
    ]
    for cp in copies:
        cp.start()
    for cp in copies:
        cp.wait()


def on_device(tokens, w_key, w_value, w_query, slot_queries, memory, norm_gain, doc_length):
    dma = pltpu.SemaphoreType.DMA
    anywhere = pl.BlockSpec(memory_space=pltpu.HBM)
    results = pl.pallas_call(
        kernel,
        out_shape=(
            pltpu.VMEM((128, 1024), BF16),
            pltpu.VMEM((256, 1024), BF16),
        ),
        in_specs=[anywhere] * 8,
        out_specs=(pl.BlockSpec(memory_space=pl.ANY),) * 2,
        scratch_shapes=[
            pltpu.VMEM((4, 512, 1024), BF16),
            pltpu.VMEM((3, 4, 4, 2, 128, 256), BF16),
            pltpu.VMEM((256, 256), BF16),
            pltpu.VMEM((32, 256), BF16),
            pltpu.VMEM((1, 256), F32),
            pltpu.SMEM((1,), jnp.int32),
            pltpu.VMEM((3, 512, 256), F32),
            pltpu.VMEM((2, 4, 32, 384), F32),
            pltpu.VMEM((4, 32, 384), F32),
            pltpu.VMEM((4, 32, 384), F32),
            pltpu.VMEM((4, 32, 384), F32),
            pltpu.VMEM((4, 4, 8, 128), F32),
            pltpu.VMEM((256, 256), BF16),
            pltpu.VMEM((32, 1024), BF16),
            pltpu.VMEM((4, 128, 256), BF16),
            dma((13,)),
            dma((2, 5)),
            dma((2, 4)),
            dma((2, 5)),
            dma((2, 4)),
            dma((4, 2, 2)),
            dma((4, 2, 2)),
            dma((2,)),
            dma((2,)),
            dma((3, 4)),
            dma((3, 4)),
            dma((3, 4, 4)),
            dma((3, 4, 4)),
            dma((3, 4)),
            dma((3, 4)),
            dma((2,)),
            dma((4,)),
            dma((4,)),
            dma((4, 4)),
            dma((4, 4)),
            dma((4, 2)),
            dma((4, 2)),
            dma((4,)),
            dma((4,)),
            dma((4,)),
            dma((4,)),
            dma((4,)),
            dma((4,)),
            dma((4,)),
            dma((4,)),
        ],
        compiler_params=pltpu.CompilerParams(
            collective_id=0, has_side_effects=True, vmem_limit_bytes=60 * 2**20
        ),
        name="luna",
    )(
        tokens, w_key, w_value, w_query, slot_queries, memory, norm_gain.reshape(1, 1024),
        doc_length,
    )
    return pl.pallas_call(
        store,
        out_shape=(
            jax.ShapeDtypeStruct((128, 1024), BF16),
            jax.ShapeDtypeStruct((256, 1024), BF16),
        ),
        in_specs=[pl.BlockSpec(memory_space=pl.ANY)] * 2,
        out_specs=(anywhere, anywhere),
        scratch_shapes=[dma((2,))],
        compiler_params=pltpu.CompilerParams(vmem_limit_bytes=2**20),
        name="store",
    )(*results)


def solution(mesh):
    in_specs = (
        P(("dp", "seq"), "head"),
        P("seq", "head"),
        P("seq", "head"),
        P("seq", "head"),
        P("dp", "head"),
        P("dp", "head"),
        P("head"),
        P("dp"),
    )
    out_specs = (P(("dp", "seq"), "head"), P("dp", "head"))
    return jax.shard_map(
        on_device, mesh=mesh, in_specs=in_specs, out_specs=out_specs, check_vma=False
    )
```

```python
import math

import jax
import jax.numpy as jnp
from jax import lax
from jax.experimental import pallas as pl
from jax.experimental.pallas import tpu as pltpu
from jax.sharding import PartitionSpec as P

D = 4096
HEAD_DIM = 128
NEGATIVE = -1e30
EPSILON = 1e-05
SCALING = 1.0 / math.sqrt(HEAD_DIM)
MESH = pl.DeviceIdType.MESH
F32 = jnp.float32
BF16 = jnp.bfloat16
NT = (((1,), (1,)), ((), ()))


def merge(pieces):
    outs, stats = [], []
    for h in range(2):
        tops = [p[:, 256 + 2 * h : 257 + 2 * h] for p in pieces]
        sums = [p[:, 257 + 2 * h : 258 + 2 * h] for p in pieces]
        accs = [p[:, h * 128 : (h + 1) * 128] for p in pieces]
        top = tops[0]
        for t in tops[1:]:
            top = jnp.maximum(top, t)
        factors = [jnp.exp(t - top) for t in tops]
        total = sum(s * f for s, f in zip(sums, factors))
        acc = sum(a * f for a, f in zip(accs, factors))
        outs.append(acc)
        stats.append((top, total))
    return outs, stats


def stat_lanes(stats, rows):
    lane = lax.broadcasted_iota(jnp.int32, (rows, 128), 1)
    (m0, s0), (m1, s1) = stats
    return jnp.where(lane == 0, m0, jnp.where(lane == 1, s0, jnp.where(lane == 2, m1, s1)))


def kernel(
    tok, wk, wv, wq, sq, mem, gain, dl,
    o_un, o_nm,
    tokb, wb, sqb, memb, gainb, dlb, acc, pm, pr, mg, mr, st, nmf, nx, ob,
    loc, z_s, z_r, zb_s, zb_r, xa_s, xa_r, f_s, f_r, xw_s, xw_r, yw_s, yw_r, cw_s, cw_r,
    p1, p2_s, p2_r, p3_s, p3_r, p4_s, p4_r, n_s, n_r, m_s, m_r, nc_s, nc_r, u_s, u_r,
):
    seq = lax.axis_index("seq")
    z = lax.axis_index("head")
    dp = lax.axis_index("dp")
    y, x, c = seq // 8, (seq // 2) % 4, seq % 2
    xs = [(x + d) % 4 for d in range(4)]
    ys = [(y + d) % 4 for d in range(4)]
    zs = [(z + d) % 4 for d in range(4)]

    def dev(x=x, y=y, z=z, c=c):
        return (y * 8 + x * 2 + c, z, dp)

    def remote(src, dst, send, recv, to):
        return pltpu.make_async_remote_copy(
            src_ref=src, dst_ref=dst, send_sem=send, recv_sem=recv, device_id=to,
            device_id_type=MESH,
        )

    sib = dev(c=1 - c)
    ws = (wk, wv, wq)

    def cols(i):
        return pl.ds(pl.multiple_of(i * 256, 256), 256)

    def group(i):
        return pl.ds(pl.multiple_of(i * 128, 128), 128)

    slots = pl.ds(pl.multiple_of(y * 64 + c * 32, 32), 32)
    local = [
        pltpu.make_async_copy(tok, tokb.at[z, group(x)], loc.at[0]),
        pltpu.make_async_copy(sq.at[:, cols(x)], sqb, loc.at[1]),
        pltpu.make_async_copy(mem.at[slots, cols(x)], memb, loc.at[2]),
    ]
    last = [
        pltpu.make_async_copy(gain.at[:, cols(x)], gainb, loc.at[11]),
        pltpu.make_async_copy(dl, dlb, loc.at[12]),
    ]
    for m in range(3):
        local.append(
            pltpu.make_async_copy(ws[m].at[:, cols(x)], wb.at[m, y, x, c], loc.at[3 + m])
        )
    for cp in local + last:
        cp.start()

    barrier = pltpu.get_barrier_semaphore()

    def greet(p):
        pl.semaphore_signal(barrier, inc=1, device_id=p, device_id_type=MESH)

    greet(sib)
    for d in range(1, 4):
        greet(dev(x=xs[d]))
        greet(dev(y=ys[d]))
    pl.when(z < 3)(lambda: greet(dev(z=z + 1)))
    pl.when(z > 0)(lambda: greet(dev(z=z - 1)))
    pl.semaphore_wait(barrier, 9 - z // 3 - (3 - z) // 3)

    sent = []

    def go(cp):
        cp.start()
        sent.append(cp)

    first = 1 + z % 2
    third = 3 * (1 - z // 2)
    second = 6 - z - first - third
    order = [z, first, second, third]
    onward = [None, 3 * (z // 2), 3 - z, 3 * (z // 2)]
    middle = (z + 1) // 2 == 1

    def chain(i, src_of, send, recv):
        if i == 0:
            ref = src_of(z)
            up = remote(ref, ref, send.at[0], recv.at[z], dev(z=z + 1))
            down = remote(ref, ref, send.at[1], recv.at[z], dev(z=z - 1))
            return [(z < 3, up), (z > 0, down)]
        zi = order[i]
        ref = src_of(zi)
        return [(middle, remote(ref, ref, send.at[i + 1], recv.at[zi], dev(z=onward[i])))]

    def start_chain(*args):
        for cond, cp in chain(*args):
            pl.when(cond)(cp.start)

    def finish_chain(*args):
        for cond, cp in chain(*args):
            pl.when(cond)(cp.wait_send)

    def wait_chain(i, src_of, send, recv):
        ref = src_of(order[i])
        remote(ref, ref, send.at[0], recv.at[order[i]], sib).wait_recv()

    def half_rows(xi, h):
        return pl.ds(pl.multiple_of(xi * 128 + 64 * h, 64), 64)

    A = [(lambda zi, h=h: tokb.at[zi, half_rows(x, h)], z_s.at[h], z_r.at[h]) for h in (0, 1)]
    B = [(lambda zi, h=h: tokb.at[zi, half_rows(xs[2], h)], zb_s.at[h], zb_r.at[h]) for h in (0, 1)]

    def send_w(m):
        for d in (2, 1, 3):
            go(remote(ws[m].at[:, cols(xs[d])], wb.at[m, y, x, c], xw_s.at[m, d], xw_r.at[m, x],
                      dev(x=xs[d])))

    def send_x(i, h, k):
        zi = order[i]
        ref = tokb.at[zi, half_rows(x, h)]
        go(remote(ref, ref, xa_s.at[i, h, k], xa_r.at[zi, h, k], dev(x=xs[1 + 2 * k])))

    def wait_x(i, h, k):
        zi = order[i]
        ref = tokb.at[zi, half_rows(xs[3 - 2 * k], h)]
        remote(ref, ref, xa_s.at[0, 0, 0], xa_r.at[zi, h, k], sib).wait_recv()

    def wait_block(i):
        for h in (0, 1):
            for k in (0, 1):
                if i or h == k:
                    wait_x(i, h, k)

    def send_y(m, dx, src):
        for d in (2, 1, 3):
            go(remote(src, wb.at[m, y, xs[dx], c], yw_s.at[m, d, dx], yw_r.at[m, y, xs[dx]],
                      dev(y=ys[d])))

    def spread_own(m):
        send_y(m, 0, ws[m].at[:, cols(x)])

    def spread_w(m):
        for d in (1, 3, 2):
            ref = wb.at[m, y, xs[d], c]
            remote(ref, ref, xw_s.at[m, d], xw_r.at[m, xs[d]], sib).wait_recv()
            send_y(m, d, ref)
        local[3 + m].wait()
        ref = wb.at[m, y, :, c]
        go(remote(ref, ref, cw_s.at[m, 0], cw_r.at[m, y], sib))

    def pass_w(m):
        for d in (1, 3, 2):
            for dx in range(4):
                ref = wb.at[m, ys[d], xs[dx], c]
                remote(ref, ref, yw_s.at[m, d, dx], yw_r.at[m, ys[d], xs[dx]], sib).wait_recv()
            ref = wb.at[m, ys[d], :, c]
            go(remote(ref, ref, cw_s.at[m, d], cw_r.at[m, ys[d]], sib))

    def wait_w(m):
        for d in range(4):
            ref = wb.at[m, ys[d], :, 1 - c]
            remote(ref, ref, cw_s.at[m, d], cw_r.at[m, ys[d]], sib).wait_recv()

    def project(m, zi, fresh):
        w = wb[m, zi].reshape(1024, 256)
        r = jnp.dot(tokb[zi], w, preferred_element_type=F32)
        if fresh:
            acc[m] = r
        else:
            acc[m] += r

    def link(i, h, which):
        wait_chain(i, *which[h])
        start_chain(i, *which[h])

    def forward(h):
        ref = tokb.at[z, half_rows(xs[1 + 2 * h], h)]
        go(remote(ref, ref, f_s.at[h], f_r.at[h], dev(x=xs[3 - 2 * h])))

    def far(h):
        ref = tokb.at[z, half_rows(xs[2], h)]
        remote(ref, ref, f_s.at[h], f_r.at[h], sib).wait_recv()
        start_chain(0, *B[h])

    def pass_block(i):
        for h in (0, 1):
            link(i, h, A)
            send_x(i, h, 0)
            send_x(i, h, 1)

    def pass_far(i):
        for h in (0, 1):
            link(i, h, B)

    local[0].wait()
    start_chain(0, *A[0])
    send_x(0, 0, 1)
    send_x(0, 1, 0)
    spread_own(0)
    start_chain(0, *A[1])
    send_x(0, 1, 1)
    send_x(0, 0, 0)
    spread_own(1)
    wait_x(0, 0, 1)
    forward(0)
    wait_x(0, 1, 0)
    forward(1)
    send_w(0)
    pass_block(1)
    send_w(1)
    spread_w(0)
    far(0)
    far(1)
    pass_block(2)
    pass_far(1)
    spread_w(1)
    pass_block(3)
    send_w(2)
    spread_own(2)
    pass_w(0)
    pass_far(2)
    pass_w(1)
    pass_far(3)
    spread_w(2)
    wait_w(0)
    for i in (0, 1):
        wait_block(i)
        project(0, order[i], i == 0)
    for i in (2,):
        wait_block(i)
        project(0, order[i], i == 0)
    wait_w(1)
    for i in (0, 1, 2):
        project(1, order[i], i == 0)
    for i in (3,):
        wait_block(i)
        project(0, order[i], i == 0)
        project(1, order[i], i == 0)

    local[1].wait()
    local[2].wait()
    for cp in last:
        cp.wait()
    length = dlb[0]
    j = lax.broadcasted_iota(jnp.int32, (1, 512), 1)
    valid = y * 1024 + (j // 128) * 256 + c * 128 + j % 128 < length
    stats = []
    for h in range(2):
        hc = slice(h * 128, (h + 1) * 128)
        k = acc[0, :, hc].astype(BF16)
        v = acc[1, :, hc].astype(BF16)
        s = lax.dot_general(sqb[:, hc], k, NT, preferred_element_type=F32) * SCALING
        s = jnp.where(valid, s, NEGATIVE)
        top = jnp.max(s, axis=1, keepdims=True)
        p = jnp.where(valid, jnp.exp(s - top), 0.0)
        total = jnp.sum(p, axis=1, keepdims=True)
        high = p.astype(BF16)
        low = (p - high.astype(F32)).astype(BF16)
        a = jnp.dot(high, v, preferred_element_type=F32) + jnp.dot(
            low, v, preferred_element_type=F32
        )
        for yy in range(4):
            for cc in range(2):
                r = yy * 64 + cc * 32
                pm[cc, yy, :, hc] = a[r : r + 32]
        stats.append((top, total))
    lanes = stat_lanes(stats, 256)
    for yy in range(4):
        for cc in range(2):
            r = yy * 64 + cc * 32
            pm[cc, yy, :, 256:384] = lanes[r : r + 32]

    cp = remote(pm.at[1 - c], pr, p1.at[0], p1.at[1], sib)
    go(cp)
    cp.wait_recv()
    outs, stats = merge([pm[c].reshape(128, 384), pr[...].reshape(128, 384)])
    mg[:, :, 0:128] = outs[0].reshape(4, 32, 128)
    mg[:, :, 128:256] = outs[1].reshape(4, 32, 128)
    mg[:, :, 256:384] = stat_lanes(stats, 128).reshape(4, 32, 128)
    for d in (2, 1, 3):
        go(remote(mg.at[ys[d]], mr.at[y], p2_s.at[d], p2_r.at[y], dev(y=ys[d])))

    for d in range(1, 4):
        remote(mr.at[ys[d]], mr.at[ys[d]], p2_s.at[d], p2_r.at[ys[d]], sib).wait_recv()
    outs, stats = merge([mg[y]] + [mr[ys[d]] for d in range(1, 4)])
    packed = jnp.concatenate([outs[h] / stats[h][1] for h in range(2)], axis=1)
    combined = memb[...].astype(F32) + packed
    stacked = jnp.concatenate([combined, combined * combined, jnp.zeros((64, 256), F32)], axis=0)
    sums = lax.dot_general(
        jnp.ones((8, 256), F32), stacked, NT, precision=lax.Precision.HIGHEST,
        preferred_element_type=F32,
    )
    st[x, z] = sums
    early = list(sent)
    sent.clear()
    for dz in (2, 3, 1, 0):
        for dx in (2, 1, 3, 0):
            if dx or dz:
                go(remote(st.at[x, z], st.at[x, z], p3_s.at[dx, dz], p3_r.at[x, z],
                          dev(x=xs[dx], z=zs[dz])))
    pass_w(2)
    for dz in range(4):
        for dx in range(4):
            if dx or dz:
                ref = st.at[xs[dx], zs[dz]]
                remote(ref, ref, p3_s.at[dx, dz], p3_r.at[xs[dx], zs[dz]], sib).wait_recv()
    sums = jnp.sum(st[...].reshape(16, 8, 128), axis=0)
    column = jnp.transpose(sums)[:, 0:1] / D
    mean = column[0:32]
    square = column[32:64]
    inverse = lax.rsqrt(square - mean * mean + EPSILON)
    piece = ((combined - mean) * inverse * gainb[...]).astype(BF16)
    nmf[slots] = piece
    nx[:, cols(x)] = piece
    ref = nmf.at[slots]
    for d in (2, 1, 3):
        for cc in (0, 1):
            to = dev(y=ys[d], c=(c + cc) % 2)
            go(remote(ref, ref, p4_s.at[d, cc], p4_r.at[y, c], to))
    go(remote(ref, ref, p4_s.at[0, 1], p4_r.at[y, c], sib))
    for d in (2, 1, 3):
        go(remote(ref, nx.at[:, cols(x)], n_s.at[d], n_r.at[x], dev(x=xs[d])))

    wait_w(2)
    for i in range(4):
        project(2, i, i == 0)

    for d in range(4):
        for cc in range(2):
            if d or cc:
                c2 = (c + cc) % 2
                ref = nmf.at[pl.ds(pl.multiple_of(ys[d] * 64 + c2 * 32, 32), 32)]
                remote(ref, ref, p4_s.at[d, cc], p4_r.at[ys[d], c2], sib).wait_recv()

    for d in range(1, 4):
        ref = nx.at[:, cols(xs[d])]
        remote(ref, ref, n_s.at[d], n_r.at[xs[d]], sib).wait_recv()
    final = [pltpu.make_async_copy(nx, o_nm.at[slots], loc.at[7])]
    final[0].start()
    for d in (2, 1, 3):
        go(remote(nx, o_nm.at[slots], m_s.at[d], m_r.at[y], dev(y=ys[d])))
    go(remote(nx, o_nm.at[slots], nc_s.at[0], nc_r.at[y], sib))

    r = lax.broadcasted_iota(jnp.int32, (128, 1), 0)
    for d in (2, 1, 3, 0):
        g = xs[d]
        live = y * 1024 + g * 256 + c * 128 + r < length
        for h in range(2):
            hc = slice(h * 128, (h + 1) * 128)
            q = acc[2, group(g), hc].astype(BF16)
            n = nmf[:, hc]
            s = lax.dot_general(q, n, NT, preferred_element_type=F32) * SCALING
            e = jnp.exp(s - jnp.max(s, axis=1, keepdims=True))
            probs = (e / jnp.sum(e, axis=1, keepdims=True)).astype(BF16)
            o = jnp.dot(probs, n, preferred_element_type=F32)
            ob[g, :, hc] = jnp.where(live, o, 0.0).astype(BF16)
        if d:
            go(remote(ob.at[g], o_un.at[:, cols(x)], u_s.at[d], u_r.at[x], dev(x=g)))
        else:
            cp = pltpu.make_async_copy(ob.at[g], o_un.at[:, cols(x)], loc.at[6])
            cp.start()
            final.append(cp)

    def rows_of(yi, ci):
        return o_nm.at[pl.ds(pl.multiple_of(yi * 64 + ci * 32, 32), 32)]

    for cp in early:
        cp.wait_send()
    for i in range(4):
        for h in (0, 1):
            finish_chain(i, *A[h])
            finish_chain(i, *B[h])
    for d in (1, 3, 2):
        ref = rows_of(ys[d], c)
        remote(ref, ref, m_s.at[d], m_r.at[ys[d]], sib).wait_recv()
        go(remote(ref, ref, nc_s.at[d], nc_r.at[ys[d]], sib))
    for d in range(1, 4):
        ref = o_un.at[:, cols(xs[d])]
        remote(ref, ref, u_s.at[d], u_r.at[xs[d]], sib).wait_recv()
    for d in range(4):
        ref = rows_of(ys[d], 1 - c)
        remote(ref, ref, nc_s.at[d], nc_r.at[ys[d]], sib).wait_recv()
    for cp in final:
        cp.wait()
    for cp in sent:
        cp.wait_send()


def store(a, b, out_a, out_b, sem):
    copies = [
        pltpu.make_async_copy(a, out_a, sem.at[0]),
        pltpu.make_async_copy(b, out_b, sem.at[1]),
    ]
    for cp in copies:
        cp.start()
    for cp in copies:
        cp.wait()


def on_device(tokens, w_key, w_value, w_query, slot_queries, memory, norm_gain, doc_length):
    dma = pltpu.SemaphoreType.DMA
    anywhere = pl.BlockSpec(memory_space=pltpu.HBM)
    results = pl.pallas_call(
        kernel,
        out_shape=(
            pltpu.VMEM((128, 1024), BF16),
            pltpu.VMEM((256, 1024), BF16),
        ),
        in_specs=[anywhere] * 8,
        out_specs=(pl.BlockSpec(memory_space=pl.ANY),) * 2,
        scratch_shapes=[
            pltpu.VMEM((4, 512, 1024), BF16),
            pltpu.VMEM((3, 4, 4, 2, 128, 256), BF16),
            pltpu.VMEM((256, 256), BF16),
            pltpu.VMEM((32, 256), BF16),
            pltpu.VMEM((1, 256), F32),
            pltpu.SMEM((1,), jnp.int32),
            pltpu.VMEM((3, 512, 256), F32),
            pltpu.VMEM((2, 4, 32, 384), F32),
            pltpu.VMEM((4, 32, 384), F32),
            pltpu.VMEM((4, 32, 384), F32),
            pltpu.VMEM((4, 32, 384), F32),
            pltpu.VMEM((4, 4, 8, 128), F32),
            pltpu.VMEM((256, 256), BF16),
            pltpu.VMEM((32, 1024), BF16),
            pltpu.VMEM((4, 128, 256), BF16),
            dma((13,)),
            dma((2, 5)),
            dma((2, 4)),
            dma((2, 5)),
            dma((2, 4)),
            dma((4, 2, 2)),
            dma((4, 2, 2)),
            dma((2,)),
            dma((2,)),
            dma((3, 4)),
            dma((3, 4)),
            dma((3, 4, 4)),
            dma((3, 4, 4)),
            dma((3, 4)),
            dma((3, 4)),
            dma((2,)),
            dma((4,)),
            dma((4,)),
            dma((4, 4)),
            dma((4, 4)),
            dma((4, 2)),
            dma((4, 2)),
            dma((4,)),
            dma((4,)),
            dma((4,)),
            dma((4,)),
            dma((4,)),
            dma((4,)),
            dma((4,)),
            dma((4,)),
        ],
        compiler_params=pltpu.CompilerParams(
            collective_id=0, has_side_effects=True, vmem_limit_bytes=60 * 2**20
        ),
        name="luna",
    )(
        tokens, w_key, w_value, w_query, slot_queries, memory, norm_gain.reshape(1, 1024),
        doc_length,
    )
    return pl.pallas_call(
        store,
        out_shape=(
            jax.ShapeDtypeStruct((128, 1024), BF16),
            jax.ShapeDtypeStruct((256, 1024), BF16),
        ),
        in_specs=[pl.BlockSpec(memory_space=pl.ANY)] * 2,
        out_specs=(anywhere, anywhere),
        scratch_shapes=[dma((2,))],
        compiler_params=pltpu.CompilerParams(vmem_limit_bytes=2**20),
        name="store",
    )(*results)


def solution(mesh):
    in_specs = (
        P(("dp", "seq"), "head"),
        P("seq", "head"),
        P("seq", "head"),
        P("seq", "head"),
        P("dp", "head"),
        P("dp", "head"),
        P("head"),
        P("dp"),
    )
    out_specs = (P(("dp", "seq"), "head"), P("dp", "head"))
    return jax.shard_map(
        on_device, mesh=mesh, in_specs=in_specs, out_specs=out_specs, check_vma=False
    )
```

```python
import math

import jax
import jax.numpy as jnp
from jax import lax
from jax.experimental import pallas as pl
from jax.experimental.pallas import tpu as pltpu
from jax.sharding import PartitionSpec as P

D = 4096
HEAD_DIM = 128
NEGATIVE = -1e30
EPSILON = 1e-05
SCALING = 1.0 / math.sqrt(HEAD_DIM)
MESH = pl.DeviceIdType.MESH
F32 = jnp.float32
BF16 = jnp.bfloat16
NT = (((1,), (1,)), ((), ()))


def merge(pieces):
    outs, stats = [], []
    for h in range(2):
        tops = [p[:, 256 + 2 * h : 257 + 2 * h] for p in pieces]
        sums = [p[:, 257 + 2 * h : 258 + 2 * h] for p in pieces]
        accs = [p[:, h * 128 : (h + 1) * 128] for p in pieces]
        top = tops[0]
        for t in tops[1:]:
            top = jnp.maximum(top, t)
        factors = [jnp.exp(t - top) for t in tops]
        total = sum(s * f for s, f in zip(sums, factors))
        acc = sum(a * f for a, f in zip(accs, factors))
        outs.append(acc)
        stats.append((top, total))
    return outs, stats


def stat_lanes(stats, rows):
    lane = lax.broadcasted_iota(jnp.int32, (rows, 128), 1)
    (m0, s0), (m1, s1) = stats
    return jnp.where(lane == 0, m0, jnp.where(lane == 1, s0, jnp.where(lane == 2, m1, s1)))


def kernel(
    tok, wk, wv, wq, sq, mem, gain, dl,
    o_un, o_nm,
    tokb, wb, sqb, memb, gainb, dlb, acc, pm, pr, mg, mr, st, nmf, nx, ob,
    loc, z_s, z_r, zb_s, zb_r, xa_s, xa_r, f_s, f_r, xw_s, xw_r, yw_s, yw_r, cw_s, cw_r,
    p1, p2_s, p2_r, p3_s, p3_r, p4_s, p4_r, n_s, n_r, m_s, m_r, nc_s, nc_r, u_s, u_r,
):
    seq = lax.axis_index("seq")
    z = lax.axis_index("head")
    dp = lax.axis_index("dp")
    y, x, c = seq // 8, (seq // 2) % 4, seq % 2
    xs = [(x + d) % 4 for d in range(4)]
    ys = [(y + d) % 4 for d in range(4)]
    zs = [(z + d) % 4 for d in range(4)]

    def dev(x=x, y=y, z=z, c=c):
        return (y * 8 + x * 2 + c, z, dp)

    def remote(src, dst, send, recv, to):
        return pltpu.make_async_remote_copy(
            src_ref=src, dst_ref=dst, send_sem=send, recv_sem=recv, device_id=to,
            device_id_type=MESH,
        )

    sib = dev(c=1 - c)
    ws = (wk, wv, wq)

    def cols(i):
        return pl.ds(pl.multiple_of(i * 256, 256), 256)

    def group(i):
        return pl.ds(pl.multiple_of(i * 128, 128), 128)

    slots = pl.ds(pl.multiple_of(y * 64 + c * 32, 32), 32)
    local = [
        pltpu.make_async_copy(tok, tokb.at[z, group(x)], loc.at[0]),
        pltpu.make_async_copy(sq.at[:, cols(x)], sqb, loc.at[1]),
        pltpu.make_async_copy(mem.at[slots, cols(x)], memb, loc.at[2]),
    ]
    last = [
        pltpu.make_async_copy(gain.at[:, cols(x)], gainb, loc.at[11]),
        pltpu.make_async_copy(dl, dlb, loc.at[12]),
    ]
    for m in range(3):
        local.append(
            pltpu.make_async_copy(ws[m].at[:, cols(x)], wb.at[m, y, x, c], loc.at[3 + m])
        )
    for cp in local + last:
        cp.start()

    barrier = pltpu.get_barrier_semaphore()

    def greet(p):
        pl.semaphore_signal(barrier, inc=1, device_id=p, device_id_type=MESH)

    greet(sib)
    for d in range(1, 4):
        greet(dev(x=xs[d]))
        greet(dev(y=ys[d]))
    pl.when(z < 3)(lambda: greet(dev(z=z + 1)))
    pl.when(z > 0)(lambda: greet(dev(z=z - 1)))
    pl.semaphore_wait(barrier, 9 - z // 3 - (3 - z) // 3)

    sent = []

    def go(cp):
        cp.start()
        sent.append(cp)

    first = 1 + z % 2
    third = 3 * (1 - z // 2)
    second = 6 - z - first - third
    order = [z, first, second, third]
    onward = [None, 3 * (z // 2), 3 - z, 3 * (z // 2)]
    middle = (z + 1) // 2 == 1

    def chain(i, src_of, send, recv):
        if i == 0:
            ref = src_of(z)
            up = remote(ref, ref, send.at[0], recv.at[z], dev(z=z + 1))
            down = remote(ref, ref, send.at[1], recv.at[z], dev(z=z - 1))
            return [(z < 3, up), (z > 0, down)]
        zi = order[i]
        ref = src_of(zi)
        return [(middle, remote(ref, ref, send.at[i + 1], recv.at[zi], dev(z=onward[i])))]

    def start_chain(*args):
        for cond, cp in chain(*args):
            pl.when(cond)(cp.start)

    def finish_chain(*args):
        for cond, cp in chain(*args):
            pl.when(cond)(cp.wait_send)

    def wait_chain(i, src_of, send, recv):
        ref = src_of(order[i])
        remote(ref, ref, send.at[0], recv.at[order[i]], sib).wait_recv()

    def half_rows(xi, h):
        return pl.ds(pl.multiple_of(xi * 128 + 64 * h, 64), 64)

    A = [(lambda zi, h=h: tokb.at[zi, half_rows(x, h)], z_s.at[h], z_r.at[h]) for h in (0, 1)]
    B = [(lambda zi, h=h: tokb.at[zi, half_rows(xs[2], h)], zb_s.at[h], zb_r.at[h]) for h in (0, 1)]

    def send_w(m):
        for d in (2, 1, 3):
            go(remote(ws[m].at[:, cols(xs[d])], wb.at[m, y, x, c], xw_s.at[m, d], xw_r.at[m, x],
                      dev(x=xs[d])))

    def send_x(i, h, k):
        zi = order[i]
        ref = tokb.at[zi, half_rows(x, h)]
        go(remote(ref, ref, xa_s.at[i, h, k], xa_r.at[zi, h, k], dev(x=xs[1 + 2 * k])))

    def wait_x(i, h, k):
        zi = order[i]
        ref = tokb.at[zi, half_rows(xs[3 - 2 * k], h)]
        remote(ref, ref, xa_s.at[0, 0, 0], xa_r.at[zi, h, k], sib).wait_recv()

    def wait_block(i):
        for h in (0, 1):
            for k in (0, 1):
                if i or h == k:
                    wait_x(i, h, k)

    def send_y(m, dx, src):
        for d in (2, 1, 3):
            go(remote(src, wb.at[m, y, xs[dx], c], yw_s.at[m, d, dx], yw_r.at[m, y, xs[dx]],
                      dev(y=ys[d])))

    def spread_own(m):
        send_y(m, 0, ws[m].at[:, cols(x)])

    def spread_w(m):
        for d in (1, 3, 2):
            ref = wb.at[m, y, xs[d], c]
            remote(ref, ref, xw_s.at[m, d], xw_r.at[m, xs[d]], sib).wait_recv()
            send_y(m, d, ref)
        local[3 + m].wait()
        ref = wb.at[m, y, :, c]
        go(remote(ref, ref, cw_s.at[m, 0], cw_r.at[m, y], sib))

    def pass_w(m):
        for d in (1, 3, 2):
            for dx in range(4):
                ref = wb.at[m, ys[d], xs[dx], c]
                remote(ref, ref, yw_s.at[m, d, dx], yw_r.at[m, ys[d], xs[dx]], sib).wait_recv()
            ref = wb.at[m, ys[d], :, c]
            go(remote(ref, ref, cw_s.at[m, d], cw_r.at[m, ys[d]], sib))

    def wait_w(m):
        for d in range(4):
            ref = wb.at[m, ys[d], :, 1 - c]
            remote(ref, ref, cw_s.at[m, d], cw_r.at[m, ys[d]], sib).wait_recv()

    def project(m, zi, fresh):
        w = wb[m, zi].reshape(1024, 256)
        r = jnp.dot(tokb[zi], w, preferred_element_type=F32)
        if fresh:
            acc[m] = r
        else:
            acc[m] += r

    def link(i, h, which):
        wait_chain(i, *which[h])
        start_chain(i, *which[h])

    def forward(h):
        ref = tokb.at[z, half_rows(xs[1 + 2 * h], h)]
        go(remote(ref, ref, f_s.at[h], f_r.at[h], dev(x=xs[3 - 2 * h])))

    def far(h):
        ref = tokb.at[z, half_rows(xs[2], h)]
        remote(ref, ref, f_s.at[h], f_r.at[h], sib).wait_recv()
        start_chain(0, *B[h])

    def pass_block(i):
        for h in (0, 1):
            link(i, h, A)
            send_x(i, h, 0)
            send_x(i, h, 1)

    def pass_far(i):
        for h in (0, 1):
            link(i, h, B)

    local[0].wait()
    start_chain(0, *A[0])
    send_x(0, 0, 1)
    send_x(0, 1, 0)
    spread_own(0)
    start_chain(0, *A[1])
    send_x(0, 1, 1)
    send_x(0, 0, 0)
    spread_own(1)
    wait_x(0, 0, 1)
    forward(0)
    wait_x(0, 1, 0)
    forward(1)
    spread_own(2)
    send_w(0)
    pass_block(1)
    send_w(1)
    spread_w(0)
    far(0)
    far(1)
    pass_block(2)
    pass_far(1)
    spread_w(1)
    pass_block(3)
    send_w(2)
    pass_w(0)
    pass_far(2)
    pass_w(1)
    pass_far(3)
    spread_w(2)
    wait_w(0)
    for i in (0, 1):
        wait_block(i)
        project(0, order[i], i == 0)
    for i in (2,):
        wait_block(i)
        project(0, order[i], i == 0)
    wait_w(1)
    for i in (0, 1, 2):
        project(1, order[i], i == 0)
    for i in (3,):
        wait_block(i)
        project(0, order[i], i == 0)
        project(1, order[i], i == 0)

    local[1].wait()
    local[2].wait()
    for cp in last:
        cp.wait()
    length = dlb[0]
    j = lax.broadcasted_iota(jnp.int32, (1, 512), 1)
    valid = y * 1024 + (j // 128) * 256 + c * 128 + j % 128 < length
    stats = []
    for h in range(2):
        hc = slice(h * 128, (h + 1) * 128)
        k = acc[0, :, hc].astype(BF16)
        v = acc[1, :, hc].astype(BF16)
        s = lax.dot_general(sqb[:, hc], k, NT, preferred_element_type=F32) * SCALING
        s = jnp.where(valid, s, NEGATIVE)
        top = jnp.max(s, axis=1, keepdims=True)
        p = jnp.where(valid, jnp.exp(s - top), 0.0)
        total = jnp.sum(p, axis=1, keepdims=True)
        high = p.astype(BF16)
        low = (p - high.astype(F32)).astype(BF16)
        a = jnp.dot(high, v, preferred_element_type=F32) + jnp.dot(
            low, v, preferred_element_type=F32
        )
        for yy in range(4):
            for cc in range(2):
                r = yy * 64 + cc * 32
                pm[cc, yy, :, hc] = a[r : r + 32]
        stats.append((top, total))
    lanes = stat_lanes(stats, 256)
    for yy in range(4):
        for cc in range(2):
            r = yy * 64 + cc * 32
            pm[cc, yy, :, 256:384] = lanes[r : r + 32]

    cp = remote(pm.at[1 - c], pr, p1.at[0], p1.at[1], sib)
    go(cp)
    cp.wait_recv()
    outs, stats = merge([pm[c].reshape(128, 384), pr[...].reshape(128, 384)])
    mg[:, :, 0:128] = outs[0].reshape(4, 32, 128)
    mg[:, :, 128:256] = outs[1].reshape(4, 32, 128)
    mg[:, :, 256:384] = stat_lanes(stats, 128).reshape(4, 32, 128)
    for d in (2, 1, 3):
        go(remote(mg.at[ys[d]], mr.at[y], p2_s.at[d], p2_r.at[y], dev(y=ys[d])))

    for d in range(1, 4):
        remote(mr.at[ys[d]], mr.at[ys[d]], p2_s.at[d], p2_r.at[ys[d]], sib).wait_recv()
    outs, stats = merge([mg[y]] + [mr[ys[d]] for d in range(1, 4)])
    packed = jnp.concatenate([outs[h] / stats[h][1] for h in range(2)], axis=1)
    combined = memb[...].astype(F32) + packed
    stacked = jnp.concatenate([combined, combined * combined, jnp.zeros((64, 256), F32)], axis=0)
    sums = lax.dot_general(
        jnp.ones((8, 256), F32), stacked, NT, precision=lax.Precision.HIGHEST,
        preferred_element_type=F32,
    )
    st[x, z] = sums
    early = list(sent)
    sent.clear()
    for dz in (2, 3, 1, 0):
        for dx in (2, 1, 3, 0):
            if dx or dz:
                go(remote(st.at[x, z], st.at[x, z], p3_s.at[dx, dz], p3_r.at[x, z],
                          dev(x=xs[dx], z=zs[dz])))
    pass_w(2)
    for dz in range(4):
        for dx in range(4):
            if dx or dz:
                ref = st.at[xs[dx], zs[dz]]
                remote(ref, ref, p3_s.at[dx, dz], p3_r.at[xs[dx], zs[dz]], sib).wait_recv()
    sums = jnp.sum(st[...].reshape(16, 8, 128), axis=0)
    column = jnp.transpose(sums)[:, 0:1] / D
    mean = column[0:32]
    square = column[32:64]
    inverse = lax.rsqrt(square - mean * mean + EPSILON)
    piece = ((combined - mean) * inverse * gainb[...]).astype(BF16)
    nmf[slots] = piece
    nx[:, cols(x)] = piece
    ref = nmf.at[slots]
    for d in (2, 1, 3):
        for cc in (0, 1):
            to = dev(y=ys[d], c=(c + cc) % 2)
            go(remote(ref, ref, p4_s.at[d, cc], p4_r.at[y, c], to))
    go(remote(ref, ref, p4_s.at[0, 1], p4_r.at[y, c], sib))
    for d in (2, 1, 3):
        go(remote(ref, nx.at[:, cols(x)], n_s.at[d], n_r.at[x], dev(x=xs[d])))

    wait_w(2)
    for i in range(4):
        project(2, i, i == 0)

    for d in range(4):
        for cc in range(2):
            if d or cc:
                c2 = (c + cc) % 2
                ref = nmf.at[pl.ds(pl.multiple_of(ys[d] * 64 + c2 * 32, 32), 32)]
                remote(ref, ref, p4_s.at[d, cc], p4_r.at[ys[d], c2], sib).wait_recv()

    for d in range(1, 4):
        ref = nx.at[:, cols(xs[d])]
        remote(ref, ref, n_s.at[d], n_r.at[xs[d]], sib).wait_recv()
    final = [pltpu.make_async_copy(nx, o_nm.at[slots], loc.at[7])]
    final[0].start()
    for d in (2, 1, 3):
        go(remote(nx, o_nm.at[slots], m_s.at[d], m_r.at[y], dev(y=ys[d])))
    go(remote(nx, o_nm.at[slots], nc_s.at[0], nc_r.at[y], sib))

    r = lax.broadcasted_iota(jnp.int32, (128, 1), 0)
    for d in (2, 1, 3, 0):
        g = xs[d]
        live = y * 1024 + g * 256 + c * 128 + r < length
        for h in range(2):
            hc = slice(h * 128, (h + 1) * 128)
            q = acc[2, group(g), hc].astype(BF16)
            n = nmf[:, hc]
            s = lax.dot_general(q, n, NT, preferred_element_type=F32) * SCALING
            e = jnp.exp(s - jnp.max(s, axis=1, keepdims=True))
            probs = (e / jnp.sum(e, axis=1, keepdims=True)).astype(BF16)
            o = jnp.dot(probs, n, preferred_element_type=F32)
            ob[g, :, hc] = jnp.where(live, o, 0.0).astype(BF16)
        if d:
            go(remote(ob.at[g], o_un.at[:, cols(x)], u_s.at[d], u_r.at[x], dev(x=g)))
        else:
            cp = pltpu.make_async_copy(ob.at[g], o_un.at[:, cols(x)], loc.at[6])
            cp.start()
            final.append(cp)

    def rows_of(yi, ci):
        return o_nm.at[pl.ds(pl.multiple_of(yi * 64 + ci * 32, 32), 32)]

    for cp in early:
        cp.wait_send()
    for i in range(4):
        for h in (0, 1):
            finish_chain(i, *A[h])
            finish_chain(i, *B[h])
    for d in (1, 3, 2):
        ref = rows_of(ys[d], c)
        remote(ref, ref, m_s.at[d], m_r.at[ys[d]], sib).wait_recv()
        go(remote(ref, ref, nc_s.at[d], nc_r.at[ys[d]], sib))
    for d in range(1, 4):
        ref = o_un.at[:, cols(xs[d])]
        remote(ref, ref, u_s.at[d], u_r.at[xs[d]], sib).wait_recv()
    for d in range(4):
        ref = rows_of(ys[d], 1 - c)
        remote(ref, ref, nc_s.at[d], nc_r.at[ys[d]], sib).wait_recv()
    for cp in final:
        cp.wait()
    for cp in sent:
        cp.wait_send()


def store(a, b, out_a, out_b, sem):
    copies = [
        pltpu.make_async_copy(a, out_a, sem.at[0]),
        pltpu.make_async_copy(b, out_b, sem.at[1]),
    ]
    for cp in copies:
        cp.start()
    for cp in copies:
        cp.wait()


def on_device(tokens, w_key, w_value, w_query, slot_queries, memory, norm_gain, doc_length):
    dma = pltpu.SemaphoreType.DMA
    anywhere = pl.BlockSpec(memory_space=pltpu.HBM)
    results = pl.pallas_call(
        kernel,
        out_shape=(
            pltpu.VMEM((128, 1024), BF16),
            pltpu.VMEM((256, 1024), BF16),
        ),
        in_specs=[anywhere] * 8,
        out_specs=(pl.BlockSpec(memory_space=pl.ANY),) * 2,
        scratch_shapes=[
            pltpu.VMEM((4, 512, 1024), BF16),
            pltpu.VMEM((3, 4, 4, 2, 128, 256), BF16),
            pltpu.VMEM((256, 256), BF16),
            pltpu.VMEM((32, 256), BF16),
            pltpu.VMEM((1, 256), F32),
            pltpu.SMEM((1,), jnp.int32),
            pltpu.VMEM((3, 512, 256), F32),
            pltpu.VMEM((2, 4, 32, 384), F32),
            pltpu.VMEM((4, 32, 384), F32),
            pltpu.VMEM((4, 32, 384), F32),
            pltpu.VMEM((4, 32, 384), F32),
            pltpu.VMEM((4, 4, 8, 128), F32),
            pltpu.VMEM((256, 256), BF16),
            pltpu.VMEM((32, 1024), BF16),
            pltpu.VMEM((4, 128, 256), BF16),
            dma((13,)),
            dma((2, 5)),
            dma((2, 4)),
            dma((2, 5)),
            dma((2, 4)),
            dma((4, 2, 2)),
            dma((4, 2, 2)),
            dma((2,)),
            dma((2,)),
            dma((3, 4)),
            dma((3, 4)),
            dma((3, 4, 4)),
            dma((3, 4, 4)),
            dma((3, 4)),
            dma((3, 4)),
            dma((2,)),
            dma((4,)),
            dma((4,)),
            dma((4, 4)),
            dma((4, 4)),
            dma((4, 2)),
            dma((4, 2)),
            dma((4,)),
            dma((4,)),
            dma((4,)),
            dma((4,)),
            dma((4,)),
            dma((4,)),
            dma((4,)),
            dma((4,)),
        ],
        compiler_params=pltpu.CompilerParams(
            collective_id=0, has_side_effects=True, vmem_limit_bytes=60 * 2**20
        ),
        name="luna",
    )(
        tokens, w_key, w_value, w_query, slot_queries, memory, norm_gain.reshape(1, 1024),
        doc_length,
    )
    return pl.pallas_call(
        store,
        out_shape=(
            jax.ShapeDtypeStruct((128, 1024), BF16),
            jax.ShapeDtypeStruct((256, 1024), BF16),
        ),
        in_specs=[pl.BlockSpec(memory_space=pl.ANY)] * 2,
        out_specs=(anywhere, anywhere),
        scratch_shapes=[dma((2,))],
        compiler_params=pltpu.CompilerParams(vmem_limit_bytes=2**20),
        name="store",
    )(*results)


def solution(mesh):
    in_specs = (
        P(("dp", "seq"), "head"),
        P("seq", "head"),
        P("seq", "head"),
        P("seq", "head"),
        P("dp", "head"),
        P("dp", "head"),
        P("head"),
        P("dp"),
    )
    out_specs = (P(("dp", "seq"), "head"), P("dp", "head"))
    return jax.shard_map(
        on_device, mesh=mesh, in_specs=in_specs, out_specs=out_specs, check_vma=False
    )
```
